512 devices in a mesh: fsdp: 32 (over y_lo, z), expert: 16 (over x, y_hi, core).
Axes of the slice: x: 4, y: 8 (y_hi: 2, y_lo: 4; y = y_hi * 4 + y_lo), z: 8, core: 2. Of those that a mesh axis runs over, the one named last changes fastest.
Arguments:
- tokens: bfloat16 [4096, 1792], P('expert', 'fsdp'), may hold values from -6 to 6
- modulation: float32 [4, 3, 1792], replicated, may hold values from -4 to 4
- routes: int32 [4096, 2], P('expert'), may hold values from 0 to 15, all different within a row
- route_weights: float32 [4096, 2], P('expert'), may hold values from 0.2 to 1
- w_first: bfloat16 [16, 1792, 7168], P('expert', None, 'fsdp'), may hold values from -0.125 to 0.125
- w_second: bfloat16 [16, 7168, 1792], P('expert', 'fsdp'), may hold values from -0.0625 to 0.0625
- head: bfloat16 [16, 1792], P(None, 'fsdp'), may hold values from -0.125 to 0.125
- targets: float32 [4096, 16], P('expert'), may hold values from -6 to 6
- ref_err: float32 [4], replicated, may hold values from 1.5 to 4
- pair_ids: int32 [4], replicated, may hold values from 0 to 3, each once
- timesteps: int32 [2], replicated, may hold values from 0 to 999
Outputs:
- grad_tokens: bfloat16 [4096, 1792], P('expert', 'fsdp')
- loss: float32 [], replicated
The draws below stay inside these ranges and needn't reach their ends.
Inputs may be any that keep to these rules, and one draw needn't show every extreme that they name: `routes`: each row names 2 different experts. `pair_ids`: each image once.
All inputs are finite; a program needn't handle non-finite values.
Results may differ from the reference program's by a relative error of at most 0.03.
Values may be sent and summed in bfloat16 or wider, within the bound.
No kernel may reach another device: no remote copies, remote signals or barrier semaphores. Data moves between devices by JAX's collectives and lax.ppermute only.
A program may use at most 64 MiB of HBM per device.

```python
import math
import jax
import jax.numpy as jnp
from jax import lax

D = 1792
FF = 7168
TOPK = 2
C_OUT = 16
SAMPLES = 4
TOK_DEV = 256
EXPERTS = 16
TOKENS = 4096
PAIRS = 2
CAP = 32
N_FSDP = 32
N_EXPERT = 16


def shard_levels(own_key, shape, cuts, smallest, high):
    gain, own = 1.0, jax.random.fold_in(own_key, 6)
    for dim, shards_of in cuts:
        draws = jnp.exp(jax.random.uniform(jax.random.fold_in(own, dim), (shards_of,), jnp.float32, smallest / len(cuts), high / len(cuts)))
        gain = gain * jnp.repeat(draws, shape[dim] // shards_of).reshape([-1 if axis == dim else 1 for axis in range(len(shape))])
    return gain


def different_ones(stream_key, rows, number_of, top, lift):
    sequence = jax.random.permutation(jax.random.fold_in(stream_key, 1), number_of)
    boost = sequence
    for power in range(3):
        boost = boost * boost // number_of
    boost = boost * lift // number_of
    chance = jax.random.randint(jax.random.fold_in(stream_key, 2), (rows, number_of), 0, 4096) + boost
    fixed_rows = jax.random.permutation(jax.random.fold_in(stream_key, 3), rows)[jnp.arange(number_of) % rows]
    chance = jnp.where(jnp.arange(rows)[:, None] == fixed_rows[None, :], 1 << 14, chance)
    merit = chance * number_of + jnp.arange(number_of)
    return lax.top_k(merit.astype(jnp.int32), top)[1].astype(jnp.int32)


def gaussian(key, dims, deviation, bound, shards=(), held_as=jnp.bfloat16):
    entries = jax.random.normal(key, dims, jnp.float32) * deviation
    if len(shards) > 0:
        entries = shard_levels(key, dims, shards, -0.22, 0.18) * entries
    return jnp.clip(entries, min=-bound, max=bound).astype(held_as)


def setup_inputs(seed: int = 0) -> dict:
    splits = jax.random.split(jax.random.key(seed), 12)
    return {
        "tokens": gaussian(splits[0], (TOKENS, D), 1.0, 6.0, ((0, 16), (1, 32))),
        "modulation": gaussian(splits[1], (SAMPLES, 3, D), 1.0, 4.0, (), jnp.float32),
        "routes": different_ones(splits[2], TOKENS, EXPERTS, TOPK, 1024),
        "route_weights": jnp.clip(0.2 + 0.8 * jax.random.uniform(splits[3], (TOKENS, TOPK), jnp.float32) ** shard_levels(splits[3], (TOKENS, TOPK), ((0, 16),), -0.2, 0.2), 0.2, 1.0),
        "w_first": gaussian(splits[4], (EXPERTS, D, FF), D ** -0.5, 0.125, ((0, 16), (2, 32))),
        "w_second": gaussian(splits[5], (EXPERTS, FF, D), FF ** -0.5, 0.0625, ((0, 16), (1, 32))),
        "head": gaussian(splits[6], (C_OUT, D), D ** -0.5, 0.125, ((1, 32),)),
        "targets": gaussian(splits[7], (TOKENS, C_OUT), 1.0, 6.0, ((0, 16),), jnp.float32),
        "ref_err": jnp.clip(jax.random.uniform(splits[8], (SAMPLES,), jnp.float32, 1.5, 4.0), 1.5, 4.0),
        "pair_ids": jax.random.permutation(splits[9], SAMPLES).astype(jnp.int32),
        "timesteps": jax.random.randint(splits[10], (PAIRS,), 0, 1000).astype(jnp.int32),
    }


norm_eps = 1e-06
dpo_beta = 2.0

def gelu_tanh(values):
    return jax.nn.gelu(values, approximate=True)

def gelu_backward(pre_act, upstream):
    return jax.vjp(gelu_tanh, pre_act)[1](upstream)[0]

def dpo_terms(sample_err, ref_err, pair_ids, timesteps):
    count = sample_err.shape[0]
    sample_ids = jnp.arange(count, dtype=jnp.int32)
    winners = pair_ids[0::2]
    losers = pair_ids[1::2]
    win_sel = (winners[:, None] == sample_ids[None, :]).astype(jnp.float32)
    lose_sel = (losers[:, None] == sample_ids[None, :]).astype(jnp.float32)
    excess = sample_err - ref_err
    margin = lax.optimization_barrier(jnp.sum(win_sel * excess[None, :], axis=1)) - lax.optimization_barrier(jnp.sum(lose_sel * excess[None, :], axis=1))
    fraction = timesteps.astype(jnp.float32) / 1000.0
    keep_level = jnp.cos((fraction + 0.008) / 1.008 * (math.pi / 2.0)) ** 2
    strength = dpo_beta * keep_level
    inside = -strength * margin
    loss = jnp.mean(jax.nn.softplus(-inside))
    slope = -jax.nn.sigmoid(-inside) / inside.shape[0]
    coef = lax.optimization_barrier(jnp.sum(win_sel * (-slope * strength)[:, None] + lose_sel * (slope * strength)[:, None], axis=0))
    return (loss, coef)

def slot_table(routes):
    flat_routes = routes.reshape(N_EXPERT, TOK_DEV * TOPK)
    expert_ids = jnp.arange(EXPERTS, dtype=jnp.int32)
    hits = (flat_routes[:, :, None] == expert_ids[None, None, :]).astype(jnp.int32)
    earlier = jnp.cumsum(hits, axis=1) - hits
    return lax.optimization_barrier(jnp.sum(earlier * hits, axis=2)).reshape(TOKENS, TOPK)

def blockwise_sum(left_blocks, right_blocks, slot_total):

    def add_block(total, pair):
        part = jnp.dot(pair[0], pair[1], preferred_element_type=jnp.float32).astype(jnp.bfloat16)
        part = lax.optimization_barrier(part)
        return (total + part.astype(jnp.float32), None)
    total, _ = lax.scan(add_block, jnp.zeros((slot_total, D), jnp.float32), (left_blocks, right_blocks))
    return total.astype(jnp.bfloat16)

def expert_forward(buffer_rows, first_weight, second_weight):
    slot_total = N_EXPERT * CAP
    hid_dev = FF // N_FSDP
    pre_act = jnp.dot(buffer_rows, first_weight, preferred_element_type=jnp.float32)
    activation = gelu_tanh(pre_act).astype(jnp.bfloat16)
    act_blocks = activation.reshape(slot_total, N_FSDP, hid_dev).transpose(1, 0, 2)
    weight_blocks = second_weight.reshape(N_FSDP, hid_dev, D)
    return (pre_act, blockwise_sum(act_blocks, weight_blocks, slot_total))

def expert_backward(pre_act, grad_rows, first_weight, second_weight):
    slot_total = N_EXPERT * CAP
    hid_dev = FF // N_FSDP
    grad_act = jnp.dot(grad_rows, second_weight.T, preferred_element_type=jnp.float32)
    grad_pre = gelu_backward(pre_act, grad_act).astype(jnp.bfloat16)
    pre_blocks = grad_pre.reshape(slot_total, N_FSDP, hid_dev).transpose(1, 0, 2)
    weight_blocks = first_weight.T.reshape(N_FSDP, hid_dev, D)
    return blockwise_sum(pre_blocks, weight_blocks, slot_total)

def reference(tokens, modulation, routes, route_weights, w_first, w_second, head, targets, ref_err, pair_ids, timesteps):
    highest = lax.Precision.HIGHEST
    slot_total = N_EXPERT * CAP
    tok_sample = TOKENS // SAMPLES
    tok_float = tokens.astype(jnp.float32)
    rms_scale = lax.rsqrt(lax.optimization_barrier(jnp.mean(tok_float * tok_float, axis=1)) + norm_eps)
    sample_of = jnp.arange(TOKENS, dtype=jnp.int32) // tok_sample
    shift_rows = modulation[sample_of, 0]
    scale_rows = modulation[sample_of, 1]
    gate_rows = modulation[sample_of, 2]
    normed_base = tok_float * rms_scale[:, None]
    normed = (normed_base * (1.0 + scale_rows) + shift_rows).astype(jnp.bfloat16)
    slots = slot_table(routes)
    group_of = jnp.arange(TOKENS, dtype=jnp.int32) // TOK_DEV
    kept = slots < CAP
    dest = jnp.where(kept, (routes * N_EXPERT + group_of[:, None]) * CAP + slots, EXPERTS * slot_total).astype(jnp.int32)
    flat_dest = dest.reshape(-1)
    buffer = jnp.zeros((EXPERTS * slot_total, D), jnp.bfloat16)
    buffer = buffer.at[flat_dest].set(jnp.repeat(normed, TOPK, axis=0), mode='drop')
    pre_all, out_all = lax.map(lambda items: expert_forward(items[0], items[1], items[2]), (buffer.reshape(EXPERTS, slot_total, D), w_first, w_second))
    out_padded = jnp.concatenate([out_all.reshape(EXPERTS * slot_total, D), jnp.zeros((1, D), jnp.bfloat16)], axis=0)
    picked = out_padded[dest].astype(jnp.float32)
    moe_out = lax.optimization_barrier(jnp.sum(route_weights[:, :, None] * picked, axis=1))
    block_out = (tok_float + gate_rows * moe_out).astype(jnp.bfloat16)
    prediction = jnp.dot(block_out, head.T, preferred_element_type=jnp.float32)
    residue = prediction - targets
    token_err = lax.optimization_barrier(jnp.sum(residue * residue, axis=1))
    sample_err = lax.optimization_barrier(jnp.sum(token_err.reshape(SAMPLES, tok_sample), axis=1)) / (tok_sample * C_OUT)
    loss, coef = dpo_terms(sample_err, ref_err, pair_ids, timesteps)
    grad_pred = TOKENS * C_OUT * coef[sample_of][:, None] * 2.0 * residue / (tok_sample * C_OUT)
    grad_block = jnp.dot(grad_pred, head.astype(jnp.float32), precision=highest)
    grad_moe = gate_rows * grad_block
    grad_values = (route_weights[:, :, None] * grad_moe[:, None, :]).reshape(TOKENS * TOPK, D)
    grad_buffer = jnp.zeros((EXPERTS * slot_total, D), jnp.float32).at[flat_dest].set(grad_values, mode='drop').astype(jnp.bfloat16)
    grad_in = lax.map(lambda items: expert_backward(items[0], items[1], items[2], items[3]), (pre_all, grad_buffer.reshape(EXPERTS, slot_total, D), w_first, w_second))
    grad_padded = jnp.concatenate([grad_in.reshape(EXPERTS * slot_total, D), jnp.zeros((1, D), jnp.bfloat16)], axis=0)
    grad_normed = lax.optimization_barrier(jnp.sum(grad_padded[dest].astype(jnp.float32), axis=1))
    scaled_grad = grad_normed * (1.0 + scale_rows)
    row_dot = lax.optimization_barrier(jnp.mean(scaled_grad * normed_base, axis=1))
    grad_norm = rms_scale[:, None] * (scaled_grad - normed_base * row_dot[:, None])
    grad_tokens = (grad_block + grad_norm).astype(jnp.bfloat16)
    return (grad_tokens, loss)
```

```python
import math

import jax
import jax.numpy as jnp
from jax import lax
from jax.sharding import PartitionSpec as P

D = 1792
TOPK = 2
C_OUT = 16
SAMPLES = 4
LANES = 128


norm_eps = 1e-06
dpo_beta = 2.0
bf16 = jnp.bfloat16
f32 = jnp.float32
highest = lax.Precision.HIGHEST
contract_first = (((0,), (0,)), ((), ()))
contract_last = (((1,), (1,)), ((), ()))


def gelu_tanh(values):
    return jax.nn.gelu(values, approximate=True)


def dpo_terms(sample_err, ref_err, pair_ids, timesteps):
    count = sample_err.shape[0]
    sample_ids = jnp.arange(count, dtype=jnp.int32)
    winners = pair_ids[0::2]
    losers = pair_ids[1::2]
    win_sel = (winners[:, None] == sample_ids[None, :]).astype(f32)
    lose_sel = (losers[:, None] == sample_ids[None, :]).astype(f32)
    excess = sample_err - ref_err
    margin = jnp.sum(win_sel * excess[None, :], axis=1) - jnp.sum(
        lose_sel * excess[None, :], axis=1
    )
    fraction = timesteps.astype(f32) / 1000.0
    keep_level = jnp.cos((fraction + 0.008) / 1.008 * (math.pi / 2.0)) ** 2
    strength = dpo_beta * keep_level
    inside = -strength * margin
    loss = jnp.mean(jax.nn.softplus(-inside))
    slope = -jax.nn.sigmoid(-inside) / inside.shape[0]
    coef = jnp.sum(
        win_sel * (-slope * strength)[:, None] + lose_sel * (slope * strength)[:, None], axis=0
    )
    return (loss, coef)


def local_slots(routes, num_experts):
    flat_routes = routes.reshape(-1)
    expert_ids = jnp.arange(num_experts, dtype=jnp.int32)
    hits = (flat_routes[:, None] == expert_ids[None, :]).astype(jnp.int32)
    earlier = jnp.cumsum(hits, axis=0) - hits
    return jnp.sum(earlier * hits, axis=1).reshape(routes.shape)


def high_low(values):
    high = lax.reduce_precision(values, exponent_bits=8, mantissa_bits=7)
    return high.astype(bf16), (values - high).astype(bf16)


def swap(chunks, axis):
    return lax.all_to_all(chunks, axis, split_axis=0, concat_axis=0, tiled=True)


def local(
    tokens,
    modulation,
    routes,
    route_weights,
    w_first,
    w_second,
    head,
    targets,
    ref_err,
    pair_ids,
    timesteps,
):
    tok_rows, feat_dev = tokens.shape
    groups = lax.axis_size("expert")
    shards = lax.axis_size("fsdp")
    capacity = TOPK * tok_rows // groups
    slot_total = groups * capacity
    tokens_all = tok_rows * groups
    tok_sample = tokens_all // SAMPLES
    my_sample = lax.axis_index("expert") * tok_rows // tok_sample
    w_in = w_first[0]
    w_out = w_second[0]
    shift, scale, gate = modulation[:, 0], modulation[:, 1], modulation[:, 2]

    with jax.named_scope("routing"):
        slots = local_slots(routes, groups)
        kept = slots < capacity
        dest = routes * capacity + slots
        slot_ids = jnp.arange(slot_total, dtype=jnp.int32)
        place = (dest[:, :, None] == slot_ids[None, None, :]) & kept[:, :, None]
        pick = jnp.any(place, axis=1).astype(bf16)
        weighted = jnp.sum(jnp.where(place, route_weights[:, :, None], 0.0), axis=1)

    with jax.named_scope("dispatch"):
        outgoing = lax.dot_general(
            pick, tokens, contract_first, preferred_element_type=f32
        ).astype(bf16)
        arrived = swap(outgoing.reshape(groups, capacity, feat_dev), "expert")
        arrived = arrived.reshape(SAMPLES, LANES, feat_dev).transpose(0, 2, 1)
        head_rows = jnp.pad(head, ((0, 0), (0, LANES - feat_dev)))
        parcel = jnp.concatenate([arrived.reshape(SAMPLES * feat_dev, LANES), head_rows], axis=0)
        gathered = swap(jnp.broadcast_to(parcel[None], (shards,) + parcel.shape), "fsdp")

    with jax.named_scope("projection"):
        body = SAMPLES * feat_dev
        head_all = gathered[:, body : body + C_OUT, :feat_dev].transpose(1, 0, 2).reshape(C_OUT, D)
        gated_head = (gate[:, None, :] * head_all[None].astype(f32)).reshape(SAMPLES * C_OUT, D)
        gated_pair = jnp.concatenate(high_low(gated_head), axis=0)
        proj = lax.dot_general(gated_pair, w_out, contract_last, preferred_element_type=f32)
        proj = proj[: SAMPLES * C_OUT] + proj[SAMPLES * C_OUT :]
        proj = proj.reshape(SAMPLES, C_OUT, -1)
        shift_pair = jnp.concatenate(high_low(shift), axis=0)
        shift_proj = jnp.dot(shift_pair, w_in, preferred_element_type=f32)
        shift_proj = shift_proj[:SAMPLES] + shift_proj[SAMPLES:]

    with jax.named_scope("first_layer"):
        normed, rms = [], []
        for s in range(SAMPLES):
            rows = gathered[:, s * feat_dev : (s + 1) * feat_dev].reshape(D, LANES).astype(f32)
            rms_s = lax.rsqrt(jnp.sum(rows * rows, axis=0) / D + norm_eps)
            rms.append(rms_s)
            normed.append(
                (rows * rms_s[None, :] * (1.0 + scale[s])[:, None] + shift[s][:, None]).astype(bf16)
            )
        normed = jnp.concatenate(normed, axis=1)
        rms = jnp.concatenate(rms)
        pre = lax.dot_general(w_in, normed, contract_first, preferred_element_type=f32)
        act, gelu_grad = jax.vjp(gelu_tanh, pre)
        act = act.astype(bf16)

    with jax.named_scope("predict"):
        parts = []
        for s in range(SAMPLES):
            proj_pair = jnp.concatenate(high_low(proj[s]), axis=0)
            part = jnp.dot(
                proj_pair, act[:, s * LANES : (s + 1) * LANES], preferred_element_type=f32
            )
            parts.append(part[:C_OUT] + part[C_OUT:])
        parts = jnp.concatenate(parts, axis=1)
        parts = parts.reshape(C_OUT, groups, capacity).transpose(1, 0, 2)
        returned = swap(parts.reshape(groups, C_OUT * capacity // LANES, LANES), "expert")
        returned = returned.reshape(groups, C_OUT, capacity).transpose(1, 0, 2)
        returned = returned.reshape(C_OUT, slot_total)
        pred = lax.dot_general(returned, weighted, contract_last, precision=highest)
        pred = pred + lax.dot_general(head, tokens, contract_last, preferred_element_type=f32)
        pred = jnp.sum(swap(jnp.broadcast_to(pred[None], (shards,) + pred.shape), "fsdp"), axis=0)
        residue = pred - targets.T
        group_err = jnp.sum(residue * residue)

    with jax.named_scope("residue"):
        weighted_residue = jnp.dot(residue, weighted, precision=highest)
        weighted_residue = weighted_residue.reshape(C_OUT, groups, capacity).transpose(1, 0, 2)
        parcel = jnp.concatenate(
            [
                weighted_residue.reshape(groups, C_OUT * capacity),
                jnp.broadcast_to(group_err, (groups, LANES)),
            ],
            axis=1,
        )
        parcel = swap(parcel.reshape(groups, -1, LANES), "expert").reshape(groups, -1)
        sample_err = jnp.sum(parcel[:, C_OUT * capacity].reshape(SAMPLES, -1), axis=1)
        upstream = parcel[:, : C_OUT * capacity].reshape(groups, C_OUT, capacity)
        upstream = upstream.transpose(1, 0, 2).reshape(C_OUT, slot_total)

    with jax.named_scope("backward"):
        grad_act = []
        for s in range(SAMPLES):
            grad_act.append(
                lax.dot_general(
                    proj[s],
                    upstream[:, s * LANES : (s + 1) * LANES],
                    contract_first,
                    precision=highest,
                )
            )
        grad_pre = gelu_grad(jnp.concatenate(grad_act, axis=1))[0]
        shift_cols = jnp.repeat(shift_proj.T, LANES, axis=1)
        row_dot = jnp.sum(grad_pre * (pre - shift_cols), axis=0)
        inner_high, inner_low = high_low((rms * rms * row_dot / D).reshape(SAMPLES, LANES))
        grad_in = jnp.dot(w_in, grad_pre.astype(bf16), preferred_element_type=f32)
        grad_in = (grad_in * rms[None, :]).astype(bf16)
        grad_in = grad_in.reshape(shards, feat_dev, SAMPLES, LANES).transpose(0, 2, 1, 3)
        parcel = jnp.concatenate(
            [
                grad_in.reshape(shards, SAMPLES * feat_dev, LANES),
                jnp.broadcast_to(inner_high[None], (shards, SAMPLES, LANES)),
                jnp.broadcast_to(inner_low[None], (shards, SAMPLES, LANES)),
            ],
            axis=1,
        )
        summed = jnp.sum(swap(parcel, "fsdp").astype(f32), axis=0)
        inner = summed[body : body + SAMPLES] + summed[body + SAMPLES : body + 2 * SAMPLES]
        inner_high, inner_low = high_low(inner)
        home = jnp.concatenate(
            [
                summed[:body].reshape(SAMPLES, feat_dev, LANES).astype(bf16),
                inner_high[:, None, :],
                inner_low[:, None, :],
            ],
            axis=1,
        )
        home = home.reshape(SAMPLES, feat_dev + 2, groups // SAMPLES, capacity)
        home = home.transpose(0, 2, 3, 1).reshape(groups, capacity, feat_dev + 2)
        home = swap(home, "expert").reshape(slot_total, feat_dev + 2)
        back = jnp.dot(pick, home, preferred_element_type=f32)

    with jax.named_scope("finish"):
        loss, coef = dpo_terms(
            sample_err / (tok_sample * C_OUT), ref_err, pair_ids, timesteps
        )
        feat_start = lax.axis_index("fsdp") * feat_dev
        my_scale = lax.dynamic_slice(scale, (my_sample, feat_start), (1, feat_dev))
        my_coef = lax.dynamic_slice(coef, (my_sample,), (1,))[0]
        my_coef = my_coef * (tokens_all * C_OUT * 2.0 / (tok_sample * C_OUT))
        grad_block = lax.dot_general(
            residue, head.astype(f32), contract_first, precision=highest
        )
        inner = back[:, feat_dev] + back[:, feat_dev + 1]
        grad_tokens = my_coef * (
            grad_block
            + back[:, :feat_dev] * (1.0 + my_scale)
            - tokens.astype(f32) * inner[:, None]
        )
    return (grad_tokens.astype(bf16), loss)


def solution(mesh):
    in_specs = (
        P("expert", "fsdp"),
        P(),
        P("expert", None),
        P("expert", None),
        P("expert", None, "fsdp"),
        P("expert", "fsdp", None),
        P(None, "fsdp"),
        P("expert", None),
        P(),
        P(),
        P(),
    )
    out_specs = (P("expert", "fsdp"), P())
    return jax.shard_map(local, mesh=mesh, in_specs=in_specs, out_specs=out_specs, check_vma=False)
```

```python
import math

import jax
import jax.numpy as jnp
from jax import lax
from jax.sharding import Mesh, PartitionSpec as P

D = 1792
TOPK = 2
C_OUT = 16
SAMPLES = 4
LANES = 128
ATTRS = 64
FSDP = ("yh", "yl", "zh", "zl")


norm_eps = 1e-06
dpo_beta = 2.0
bf16 = jnp.bfloat16
f32 = jnp.float32
highest = lax.Precision.HIGHEST
contract_first = (((0,), (0,)), ((), ()))
contract_last = (((1,), (1,)), ((), ()))


def gelu_tanh(values):
    return jax.nn.gelu(values, approximate=True)


def dpo_terms(sample_err, ref_err, pair_ids, timesteps):
    count = sample_err.shape[0]
    sample_ids = jnp.arange(count, dtype=jnp.int32)
    winners = pair_ids[0::2]
    losers = pair_ids[1::2]
    win_sel = (winners[:, None] == sample_ids[None, :]).astype(f32)
    lose_sel = (losers[:, None] == sample_ids[None, :]).astype(f32)
    excess = sample_err - ref_err
    margin = jnp.sum(win_sel * excess[None, :], axis=1) - jnp.sum(
        lose_sel * excess[None, :], axis=1
    )
    fraction = timesteps.astype(f32) / 1000.0
    keep_level = jnp.cos((fraction + 0.008) / 1.008 * (math.pi / 2.0)) ** 2
    strength = dpo_beta * keep_level
    inside = -strength * margin
    loss = jnp.mean(jax.nn.softplus(-inside))
    slope = -jax.nn.sigmoid(-inside) / inside.shape[0]
    coef = jnp.sum(
        win_sel * (-slope * strength)[:, None] + lose_sel * (slope * strength)[:, None], axis=0
    )
    return (loss, coef)


def local_slots(routes, num_experts):
    flat_routes = routes.reshape(-1)
    expert_ids = jnp.arange(num_experts, dtype=jnp.int32)
    hits = (flat_routes[:, None] == expert_ids[None, :]).astype(jnp.int32)
    earlier = jnp.cumsum(hits, axis=0) - hits
    return jnp.sum(earlier * hits, axis=1).reshape(routes.shape)


def high_low(values):
    high = lax.reduce_precision(values, exponent_bits=8, mantissa_bits=7)
    return high.astype(bf16), (values - high).astype(bf16)


def swap(chunks, axis):
    return lax.all_to_all(chunks, axis, split_axis=0, concat_axis=0, tiled=True)


def copies(part, count):
    return jnp.broadcast_to(part[None], (count,) + part.shape)


def trade(part, axis):
    return lax.ppermute(part, axis, [(0, 1), (1, 0)])


def local(
    tokens,
    modulation,
    routes,
    route_weights,
    w_first,
    w_second,
    head,
    targets,
    ref_err,
    pair_ids,
    timesteps,
):
    tok_rows, feat_dev = tokens.shape
    groups = lax.axis_size("expert")
    shards = lax.axis_size(FSDP)
    capacity = TOPK * tok_rows // groups
    slot_total = groups * capacity
    tokens_all = tok_rows * groups
    tok_sample = tokens_all // SAMPLES
    block = tok_rows // shards
    my_shard = lax.axis_index(FSDP)
    my_sample = lax.axis_index("expert") * tok_rows // tok_sample
    quarter = lax.axis_index(("yl", "zl"))
    leader = (lax.axis_index(("yh", "zh")) == 0).astype(f32)
    sharers = lax.axis_size(("yh", "zh"))
    head_rows = C_OUT * feat_dev // LANES
    w_in = w_first[0]
    w_out = w_second[0]

    with jax.named_scope("weights"):
        half = D // 2
        w_y = trade(w_in, "yl")
        w_z = trade(w_in, "zl")
        w_d = jnp.concatenate([trade(w_z[:half], "yl"), trade(w_y[half:], "zl")], axis=0)
        weights = [w_in, w_y, w_z, w_d]

    with jax.named_scope("routing"):
        slots = local_slots(routes, groups)
        kept = slots < capacity
        dest = jnp.where(kept, routes * capacity + slots, -1)
        slot_ids = jnp.arange(slot_total, dtype=jnp.int32)
        place = (dest.T.reshape(-1)[:, None] == slot_ids[None, :]).astype(bf16)
        pick = place[:tok_rows] + place[tok_rows:]
        kept_w = jnp.where(kept, route_weights, 0.0)
        other_e = jnp.where(kept, routes, 0).astype(f32)
        other_s = jnp.where(kept, slots, 0).astype(f32)
        first = jnp.stack([jnp.ones((tok_rows,), f32), 1.0 - kept[:, 0].astype(f32)])
        target_parts = jnp.concatenate(high_low(targets.T), axis=0)
        rows = list(high_low(route_weights.T.reshape(-1)))
        rows += list(high_low(kept_w[:, ::-1].T.reshape(-1)))
        rows += [other_e[:, ::-1].T.reshape(-1), other_s[:, ::-1].T.reshape(-1), first.reshape(-1)]
        rows = jnp.stack([row.astype(bf16) for row in rows])
        table = jnp.concatenate(
            [
                jnp.concatenate([target_parts, target_parts], axis=1),
                rows,
                jnp.zeros((ATTRS - 2 * C_OUT - rows.shape[0], TOPK * tok_rows), bf16),
            ],
            axis=0,
        )
        share = ATTRS // shards
        mine = lax.dynamic_slice_in_dim(table, my_shard * share, share, 0)
        flat_tokens = tokens.T
        outgoing = jnp.concatenate(
            [jnp.concatenate([flat_tokens, flat_tokens], axis=1), mine], axis=0
        )

    with jax.named_scope("dispatch"):
        width = feat_dev + share
        outgoing = jnp.dot(outgoing, place, preferred_element_type=f32).astype(bf16)
        outgoing = outgoing.reshape(width, groups, capacity).transpose(1, 0, 2)
        arrived = swap(outgoing, "expert")
        arrived = arrived.reshape(SAMPLES, groups // SAMPLES, width, capacity)
        arrived = arrived.transpose(0, 2, 1, 3).reshape(1, 2, 1, 2, width, LANES)
        base = lax.dot_general(head, tokens, contract_last, preferred_element_type=f32)
        base = base.reshape(C_OUT, shards, block).transpose(1, 0, 2).reshape(shards, LANES)
        base_high, base_low = high_low(base)
        parcel = jnp.concatenate(
            [
                jnp.broadcast_to(arrived, (2, 2, 4, 2, width, LANES)).reshape(shards, width, LANES),
                copies(head.reshape(head_rows, LANES), shards),
                base_high[:, None],
                base_low[:, None],
                jnp.zeros((shards, -(width + head_rows + 2) % 8, LANES), bf16),
            ],
            axis=1,
        )
        gathered = swap(parcel, FSDP)

    with jax.named_scope("projection"):
        at = width + head_rows
        head_all = gathered[:, width:at].reshape(shards, C_OUT, feat_dev)
        head_all = head_all.transpose(1, 0, 2).reshape(C_OUT, D)
        base = jnp.sum(gathered[:, at : at + 2].astype(f32), axis=(0, 1)).reshape(C_OUT, block)
        gated_head = modulation[:, 2][:, None, :] * head_all[None].astype(f32)
        gated_pair = jnp.concatenate(high_low(gated_head.reshape(SAMPLES * C_OUT, D)), axis=0)
        proj = lax.dot_general(gated_pair, w_out, contract_last, preferred_element_type=f32)
        proj = proj[: SAMPLES * C_OUT] + proj[SAMPLES * C_OUT :]
        proj = proj.reshape(SAMPLES, C_OUT, -1)

        def projection_of(flip):
            return lax.dynamic_index_in_dim(proj, quarter ^ flip, 0, keepdims=False)

        opposite = [(i, 3 - i) for i in range(4)]
        proj = [
            projection_of(0),
            trade(projection_of(2), "yl"),
            trade(projection_of(1), "zl"),
            lax.ppermute(projection_of(3), ("yl", "zl"), opposite),
        ]

    with jax.named_scope("first_layer"):
        mod = lax.dynamic_index_in_dim(modulation, quarter, 0, keepdims=False)
        shift = mod[0][:, None]
        scale = 1.0 + mod[1][:, None]
        rows = gathered[:, :feat_dev].reshape(D, LANES)
        row_float = rows.astype(f32)
        rms = lax.rsqrt(jnp.sum(row_float * row_float, axis=0) / D + norm_eps)
        normed = (row_float * rms[None, :] * scale + shift).astype(bf16)
        attrs = gathered[:, feat_dev:width].reshape(ATTRS, LANES).astype(f32)
        target = attrs[:C_OUT] + attrs[C_OUT : 2 * C_OUT]
        own_w = attrs[32] + attrs[33]
        other_w = attrs[34] + attrs[35]
        first = attrs[38]
        base_rows = jnp.dot(head_all, rows, preferred_element_type=f32)
        act, gelu_grad = [], []
        for weight in weights:
            pre = lax.dot_general(weight, normed, contract_first, preferred_element_type=f32)
            values, backward = jax.vjp(gelu_tanh, pre)
            act.append(values.astype(bf16))
            gelu_grad.append(backward)

    with jax.named_scope("predict"):
        part = 0.0
        for proj_block, act_block in zip(proj, act):
            proj_pair = jnp.concatenate(high_low(proj_block), axis=0)
            part = part + jnp.dot(proj_pair, act_block, preferred_element_type=f32)
        part = part[:C_OUT] + part[C_OUT:]
        own = jnp.sum(swap(copies(part, sharers), ("yh", "zh")), axis=0)
        everyone = swap(copies(own.astype(bf16), groups), "expert")
        everyone = everyone.transpose(1, 0, 2).reshape(C_OUT, groups * LANES)
        lane = jnp.arange(LANES, dtype=jnp.int32)
        source = attrs[36] * LANES + attrs[37] + (lane // capacity * capacity).astype(f32)
        source = source.astype(jnp.int32)
        chosen = jnp.arange(groups * LANES, dtype=jnp.int32)[:, None] == source[None, :]
        partner = jnp.dot(everyone, chosen.astype(bf16), preferred_element_type=f32)
        residue = base_rows + own_w * own + other_w * partner - target
        kept_err = jnp.sum(first * residue * residue)

    with jax.named_scope("dropped"):
        lost = 1.0 - jnp.any(kept, axis=1).astype(f32)
        my_lost = lax.dynamic_slice_in_dim(lost, my_shard * block, block, 0)
        my_targets = lax.dynamic_slice_in_dim(targets, my_shard * block, block, 0)
        lost_residue = (base - my_targets.T) * my_lost[None, :]
        sample_ids = jnp.arange(LANES, dtype=jnp.int32)
        err_row = jnp.where(sample_ids == quarter, leader * kept_err, 0.0)
        err_row += jnp.where(sample_ids == my_sample, jnp.sum(lost_residue * lost_residue), 0.0)

    with jax.named_scope("backward"):
        upstream = own_w * residue
        grad_in = 0.0
        for weight, proj_block, backward in zip(weights, proj, gelu_grad):
            grad_act = lax.dot_general(proj_block, upstream, contract_first, precision=highest)
            grad_pre = backward(grad_act)[0].astype(bf16)
            grad_in = grad_in + jnp.dot(weight, grad_pre, preferred_element_type=f32)
        grad_in = grad_in * (rms[None, :] * scale)
        inner = jnp.sum(grad_in * row_float, axis=0) * rms * rms / D
        direct = jnp.concatenate(high_low(first * residue / sharers), axis=0)
        direct = lax.dot_general(
            jnp.concatenate([head_all, head_all], axis=0),
            direct,
            contract_first,
            preferred_element_type=f32,
        )
        grad_rows = (grad_in - row_float * inner[None, :] + direct).astype(bf16)
        tail = jnp.stack(high_low(lost_residue.reshape(LANES)) + high_low(err_row))
        tail = jnp.concatenate([tail, jnp.zeros((4, LANES), bf16)], axis=0)
        parcel = jnp.concatenate(
            [grad_rows.reshape(shards, feat_dev, LANES), copies(tail, shards)], axis=1
        )
        parcel = swap(parcel, FSDP)
        lost_residue = parcel[:, feat_dev].astype(f32) + parcel[:, feat_dev + 1].astype(f32)
        lost_residue = lost_residue.reshape(shards, C_OUT, block)
        lost_residue = lost_residue.transpose(1, 0, 2).reshape(C_OUT, tok_rows)
        err_row = jnp.sum(
            parcel[:, feat_dev + 2 : feat_dev + 4, :SAMPLES].astype(f32), axis=(0, 1)
        )
        home = parcel[:, :feat_dev].reshape(2, 2, 4, 2, feat_dev, LANES).astype(f32)
        home = jnp.sum(home, axis=(0, 2)).astype(bf16)
        home = home.reshape(SAMPLES, feat_dev, groups // SAMPLES, capacity)
        home = home.transpose(0, 2, 1, 3).reshape(groups, feat_dev, capacity)
        tail = jnp.concatenate(high_low(err_row) + (jnp.zeros((capacity - 8,), bf16),))
        home = jnp.concatenate([home, copies(tail[None], groups)], axis=1)
        home = swap(home, "expert")
        err_row = home[:, feat_dev, :SAMPLES].astype(f32) + home[:, feat_dev, 4:8].astype(f32)
        sample_err = jnp.sum(err_row, axis=0)
        back = home[:, :feat_dev].transpose(0, 2, 1).reshape(slot_total, feat_dev)
        back = jnp.dot(pick, back, preferred_element_type=f32)

    with jax.named_scope("finish"):
        loss, coef = dpo_terms(
            sample_err / (tok_sample * C_OUT), ref_err, pair_ids, timesteps
        )
        my_coef = lax.dynamic_slice(coef, (my_sample,), (1,))[0]
        my_coef = my_coef * (tokens_all * C_OUT * 2.0 / (tok_sample * C_OUT))
        direct = lax.dot_general(
            lost_residue, head.astype(f32), contract_first, precision=highest
        )
        grad_tokens = my_coef * (direct + back)
    return (grad_tokens.astype(bf16), loss)


def solution(mesh):
    mesh = Mesh(mesh.devices.reshape(2, 2, 4, 2, 16), FSDP + ("expert",))
    in_specs = (
        P("expert", FSDP),
        P(),
        P("expert", None),
        P("expert", None),
        P("expert", None, FSDP),
        P("expert", FSDP, None),
        P(None, FSDP),
        P("expert", None),
        P(),
        P(),
        P(),
    )
    out_specs = (P("expert", FSDP), P())
    return jax.shard_map(local, mesh=mesh, in_specs=in_specs, out_specs=out_specs, check_vma=False)
```

```python
import functools
import math

import jax
import jax.numpy as jnp
from jax import lax
from jax.experimental import pallas as pl
from jax.experimental.pallas import tpu as pltpu
from jax.sharding import Mesh, PartitionSpec as P

D = 1792
TOPK = 2
C_OUT = 16
SAMPLES = 4
LANES = 128
FEAT = 56
SHARDS = 32
GROUPS = 16
CAP = 32
TOK = 256
HID = 224
PACK = 64
ROWS = 72
FSDP = ("yh", "yl", "zh", "zl")
QUAD = ("yl", "zl")
SHARERS = ("yh", "zh")


norm_eps = 1e-06
dpo_beta = 2.0
bf16 = jnp.bfloat16
f32 = jnp.float32
i32 = jnp.int32
highest = lax.Precision.HIGHEST
contract_last = (((1,), (1,)), ((), ()))
contract_first = (((0,), (0,)), ((), ()))


def dot(a, b, **kw):
    return jnp.dot(a, b, preferred_element_type=f32, **kw)


def dot_nt(a, b, **kw):
    return lax.dot_general(a, b, contract_last, preferred_element_type=f32, **kw)


def iota(shape, axis):
    return lax.broadcasted_iota(i32, shape, axis)


def high_low(values):
    high = values.astype(bf16).astype(f32)
    return high, values - high


def whole(weight):
    if isinstance(weight, tuple):
        return jnp.concatenate([part[...] for part in weight], axis=0)
    return weight[...]


def lane_blocks(tiles):
    block = iota(tiles[0].shape, 1) // CAP
    out = []
    for b in range(4):
        total = None
        for j in range(4):
            moved = tiles[j] if j == b else pltpu.roll(tiles[j], (CAP * (j - b)) % LANES, axis=1)
            total = moved if total is None else jnp.where(block == j, moved, total)
        out.append(total)
    return out


def routing_kernel(
    place_ref, tokens_ref, routes_ref, weights_ref, targets_ref, head_ref,
    sent_ref, pick_ref, base_ref, facts_ref,
):
    shard = place_ref[0]
    tokens = tokens_ref[...]
    expert = iota((GROUPS, TOK), 0)
    hits = [(routes_ref[k : k + 1, :] == expert).astype(f32) for k in range(TOPK)]
    below = (iota((TOK, TOK), 0) < iota((TOK, TOK), 1)).astype(bf16)
    earlier = dot((hits[0] + hits[1]).astype(bf16), below)
    slots = [jnp.sum(earlier * hit, axis=0, keepdims=True) for hit in hits]
    kept = [(slot < CAP).astype(f32) for slot in slots]
    lane = iota((GROUPS * CAP, TOK), 0)
    places = []
    for k in range(TOPK):
        dest = jnp.where(
            kept[k] > 0.5, routes_ref[k : k + 1, :] * CAP + slots[k].astype(i32), -1
        )
        places.append((lane == dest).astype(f32))
    pick_ref[...] = (places[0] + places[1]).astype(bf16)
    pick_ref.start()

    target_high, target_low = high_low(targets_ref[...])
    row = iota((PACK, LANES), 0)
    column = iota((PACK, LANES), 1)
    pick_fact = (row >= FEAT) & (row < FEAT + 2) & (column == 2 * shard + row - FEAT)
    pick_fact = pick_fact.astype(bf16)
    body = jnp.concatenate([tokens.astype(f32), jnp.zeros((PACK - FEAT, TOK), f32)], axis=0)
    packed = None
    for k in range(TOPK):
        other = 1 - k
        own = high_low(weights_ref[k : k + 1, :])
        partner = high_low(weights_ref[other : other + 1, :] * kept[other])
        first = jnp.ones((1, TOK), f32) if k == 0 else 1.0 - kept[0]
        facts = [
            own[0], own[1], partner[0], partner[1],
            routes_ref[other : other + 1, :].astype(f32) * kept[other],
            slots[other] * kept[other],
            first,
        ]
        line = iota((8, TOK), 0)
        table = jnp.zeros((8, TOK), f32)
        for place, fact in enumerate(facts):
            table = jnp.where(line == place, fact, table)
        table = jnp.concatenate(
            [target_high, target_low, table, jnp.zeros((LANES - 40, TOK), f32)], axis=0
        )
        features = body + dot(pick_fact, table.astype(bf16))
        part = dot_nt(features.astype(bf16), places[k].astype(bf16))
        packed = part if packed is None else packed + part
    for tile in range(4):
        pieces = [
            packed[16 * j : 16 * j + 16, tile * LANES : (tile + 1) * LANES] for j in range(4)
        ]
        for b, piece in enumerate(lane_blocks(pieces)):
            sent_ref[4 * tile + b] = piece.astype(bf16)

    base = dot(head_ref[...], tokens)
    lost = (1.0 - kept[0]) * (1.0 - kept[1])
    lost = jnp.broadcast_to(lost, (C_OUT, TOK))
    stack = jnp.concatenate([base, targets_ref[...], lost], axis=0).T
    stack = jnp.concatenate([stack, jnp.zeros((TOK, LANES - 3 * C_OUT), f32)], axis=1)
    group = iota((SHARDS, LANES), 1) // C_OUT
    for place in range(3):
        total = jnp.zeros((SHARDS, LANES), f32)
        for j in range(8):
            piece = stack[SHARDS * j : SHARDS * (j + 1)]
            shift = (C_OUT * (j - place)) % LANES
            piece = pltpu.roll(piece, shift, axis=1) if shift else piece
            total = jnp.where(group == j, piece, total)
        if place == 0:
            base_ref[...] = total
        else:
            facts_ref[place - 1] = total


def parcel_kernel(arrived_ref, base_ref, head_ref, parcel_ref):
    base_high, base_low = high_low(base_ref[...])
    row = iota((8, LANES), 0)
    head = head_ref[...].astype(f32)
    for q in range(4):
        tiles = lane_blocks([arrived_ref[4 * q + b].astype(f32) for b in range(4)])
        body = jnp.concatenate([tiles[0], tiles[1], tiles[2], tiles[3][:8]], axis=0)
        last = tiles[3][8:]
        for high in range(8):
            f = (high // 4) * 16 + (q // 2) * 8 + (high % 4) * 2 + q % 2
            tail = jnp.where(row == 2, base_high[f : f + 1], last)
            tail = jnp.where(row == 3, base_low[f : f + 1], tail)
            parcel_ref[f] = jnp.concatenate([body, tail, head], axis=0).astype(bf16)


def head_kernel(gathered_ref, gate_ref, w_out_ref, proj_ref, head_ref):
    pieces = []
    for f in range(SHARDS):
        rows = gathered_ref[f, PACK:ROWS].astype(f32)
        for i in range(FEAT // 8):
            pieces.append(jnp.broadcast_to(rows[i : i + 1], (8, LANES)))
    spread = jnp.concatenate(pieces, axis=0)
    lane = iota((D, LANES), 1)
    spread = jnp.where(lane // C_OUT == iota((D, LANES), 0) % 8, spread, 0.0).astype(bf16)
    fold = iota((LANES, LANES), 0) % C_OUT == iota((LANES, LANES), 1) % C_OUT
    head = dot(spread, fold.astype(bf16))
    head_ref[...] = head.astype(bf16)
    head_ref.start()
    high, low = high_low(head * gate_ref[...])
    pair = jnp.where(lane < PACK, high, low).astype(bf16)
    proj = dot(w_out_ref[...], pair)
    proj = proj + pltpu.roll(proj, PACK, axis=1)
    proj = proj.T
    for s in range(SAMPLES):
        proj_ref[s] = proj[C_OUT * s : C_OUT * (s + 1)]


def first_kernel(
    gathered_ref, mod_ref, w0_ref, w1_ref, w2_ref, w3_ref, w4_ref, act_ref, slope_ref, rows_ref
):
    rows = jnp.concatenate([gathered_ref[f, :FEAT].astype(f32) for f in range(SHARDS)], axis=0).T
    rows_ref[...] = rows.astype(bf16)
    rows_ref.start()
    rms = lax.rsqrt(jnp.sum(rows * rows, axis=1, keepdims=True) / D + norm_eps)
    normed = (rows * rms) * (1.0 + mod_ref[1:2, :]) + mod_ref[0:1, :]
    normed = normed.astype(bf16)
    weights = [w0_ref, w1_ref, w2_ref, (w3_ref, w4_ref)]
    for b, weight in enumerate(weights):
        pre = dot_nt(normed, whole(weight))
        cubic = math.sqrt(2.0 / math.pi)
        square = pre * pre
        tanh = jnp.tanh(cubic * (pre + 0.044715 * square * pre))
        half = 0.5 * (1.0 + tanh)
        act_ref[b] = (pre * half).astype(bf16)
        slope_ref[b] = half + 0.5 * pre * (1.0 - tanh * tanh) * (
            cubic * (1.0 + 3.0 * 0.044715 * square)
        )


def predict_kernel(place_ref, act_ref, proj_ref, part_ref):
    quarter = place_ref[1]
    total = None
    for b in range(4):
        high, low = high_low(proj_ref[quarter ^ b])
        pair = jnp.concatenate([high, low], axis=0).astype(bf16)
        part = dot_nt(pair, act_ref[b])
        total = part if total is None else total + part
    total = total[:C_OUT] + total[C_OUT:]
    for other in range(8):
        part_ref[other] = total


def own_kernel(parts_ref, own_ref, shared_ref):
    own = jnp.sum(parts_ref[...], axis=0)
    own_ref[...] = own
    for e in range(GROUPS):
        shared_ref[e] = own.astype(bf16)


def base_kernel(gathered_ref, rows_ref, head_ref, base_ref, facts_ref):
    base = dot(rows_ref[...], head_ref[...]).T
    base_ref[...] = base[:C_OUT]
    tails = [gathered_ref[f, FEAT:PACK].astype(f32) for f in range(SHARDS)]
    facts = jnp.concatenate([tail[:2] for tail in tails], axis=0)
    facts_ref[:PACK] = facts
    facts_ref[PACK:] = functools.reduce(jnp.add, tails)


def backward_kernel(
    place_ref, shared_ref, own_ref, base_ref, facts_ref, block_ref, proj_ref, slope_ref,
    mod_ref, head_ref, rows_ref, w0_ref, w1_ref, w2_ref, w3_ref, w4_ref, parcel_ref,
):
    shard, quarter, leader, sample = place_ref[0], place_ref[1], place_ref[2], place_ref[3]
    facts = facts_ref[...]
    target = facts[:C_OUT] + facts[C_OUT : 2 * C_OUT]
    own_w = facts[32:33] + facts[33:34]
    other_w = facts[34:35] + facts[35:36]
    first = facts[38:39]
    lane = iota((1, LANES), 1)
    source = facts[36:37].astype(i32) * LANES + facts[37:38].astype(i32) + lane // CAP * CAP
    chosen = (iota((GROUPS * LANES, LANES), 0) == source).astype(f32).astype(bf16)
    everyone = jnp.concatenate([shared_ref[e] for e in range(GROUPS)], axis=1)
    partner = dot(everyone, chosen)
    residue = base_ref[...] + own_w * own_ref[...] + other_w * partner - target
    kept_err = jnp.sum(first * residue * residue, keepdims=True)

    lost_base = facts[PACK + 2 : PACK + 3] + facts[PACK + 3 : PACK + 4]
    lost = (lost_base - block_ref[0, pl.ds(shard, 1), :]) * block_ref[1, pl.ds(shard, 1), :]
    lost_err = jnp.sum(lost * lost, keepdims=True)
    err = jnp.where((lane == quarter) & (leader == 1), kept_err, 0.0)
    err = err + jnp.where(lane == sample, lost_err, 0.0)
    row = iota((8, LANES), 0)
    tail = jnp.zeros((8, LANES), f32)
    for place, values in enumerate(high_low(lost) + high_low(err)):
        tail = jnp.where(row == place, values, tail)

    upstream = (own_w * residue).T
    weights = [w0_ref, w1_ref, w2_ref, (w3_ref, w4_ref)]
    total = None
    for b, weight in enumerate(weights):
        grad = slope_ref[b] * dot(upstream, proj_ref[quarter ^ b], precision=highest)
        part = dot(grad.astype(bf16), whole(weight))
        total = part if total is None else total + part
    rows = rows_ref[...].astype(f32)
    rms = lax.rsqrt(jnp.sum(rows * rows, axis=1, keepdims=True) / D + norm_eps)
    total = total * (rms * (1.0 + mod_ref[1:2, :]))
    inner = jnp.sum(total * rows, axis=1, keepdims=True) * (rms * rms / D)
    high, low = high_low(first * residue * 0.125)
    direct = jnp.concatenate([high, low, jnp.zeros((LANES - 2 * C_OUT, LANES), f32)], axis=0)
    total = total - rows * inner + dot_nt(direct.T.astype(bf16), head_ref[...])
    total = total.T
    for f in range(SHARDS):
        parcel_ref[f] = jnp.concatenate(
            [total[FEAT * f : FEAT * (f + 1)], tail], axis=0
        ).astype(bf16)


def mid_kernel(parcel_ref, home_ref, lost_ref):
    lane = iota((1, LANES), 1)
    row = iota((8, LANES), 0)
    sums, tails = [], []
    for q in range(4):
        total = None
        for high in range(8):
            f = (high // 4) * 16 + (q // 2) * 8 + (high % 4) * 2 + q % 2
            part = parcel_ref[f].astype(f32)
            lost_ref[0, f : f + 1] = part[FEAT : FEAT + 1]
            lost_ref[1, f : f + 1] = part[FEAT + 1 : FEAT + 2]
            total = part if total is None else total + part
        sums.append(total[:FEAT])
        tails.append(total[FEAT:])
    tail = tails[0] + tails[1] + tails[2] + tails[3]
    err = jnp.where(lane < SAMPLES, tail[2:3] + tail[3:4], 0.0)
    err = err + pltpu.roll(err, CAP, axis=1)
    err = err + pltpu.roll(err, 2 * CAP, axis=1)
    high, low = high_low(err)
    tail = jnp.where(row == 0, high, 0.0) + jnp.where(row == 1, low, 0.0)
    for q in range(4):
        full = jnp.concatenate([sums[q], tail], axis=0)
        tiles = lane_blocks([full[16 * j : 16 * j + 16] for j in range(4)])
        for b in range(4):
            home_ref[4 * q + b] = tiles[b].astype(bf16)


def end_kernel(
    place_ref, levels_ref, home_ref, pick_ref, lost_ref, head_ref,
    grad_ref, loss_ref,
):
    sample = place_ref[3]
    pairs = [place_ref[4 + i] for i in range(SAMPLES)]
    columns = []
    for tile in range(4):
        tiles = lane_blocks([home_ref[4 * tile + b].astype(f32) for b in range(4)])
        columns.append(jnp.concatenate(tiles, axis=0))
    home = jnp.concatenate(columns, axis=1)
    back = dot(home.astype(bf16), pick_ref[...])
    err = functools.reduce(jnp.add, [column[FEAT : FEAT + 1] for column in columns])
    err = err + functools.reduce(jnp.add, [column[FEAT + 1 : FEAT + 2] for column in columns])
    err = jnp.broadcast_to(err, (8, LANES)) / (TOK * GROUPS // SAMPLES * C_OUT)
    lane = iota((8, LANES), 1) % CAP
    excess = []
    for s in range(SAMPLES):
        total = jnp.sum(jnp.where(lane == s, err, 0.0), axis=1, keepdims=True)
        excess.append(jnp.broadcast_to(total, (8, LANES)) - levels_ref[s])
    loss, coef = 0.0, 0.0
    for k in range(2):
        winner, loser = pairs[2 * k], pairs[2 * k + 1]
        margin = 0.0
        for s in range(SAMPLES):
            margin = margin + jnp.where(winner == s, excess[s], 0.0)
        for s in range(SAMPLES):
            margin = margin - jnp.where(loser == s, excess[s], 0.0)
        down = levels_ref[SAMPLES + k] * margin
        loss = loss + jnp.maximum(down, 0.0) + jnp.log1p(jnp.exp(-jnp.abs(down)))
        rate = levels_ref[SAMPLES + k] / (1.0 + jnp.exp(-down)) * 0.5
        coef = coef + jnp.where(winner == sample, rate, 0.0)
        coef = coef - jnp.where(loser == sample, rate, 0.0)
    loss_ref[...] = loss[0:1, 0:1] * 0.5
    lane = iota((SHARDS, LANES), 1) // C_OUT
    head_tile = jnp.concatenate([head_ref[...]] * 8, axis=0).astype(f32).T.astype(bf16)
    direct = 0.0
    for part in range(2):
        lost = [jnp.where(lane == j, lost_ref[part], 0.0) for j in range(8)]
        direct = direct + dot_nt(head_tile, jnp.concatenate(lost, axis=0).astype(bf16))
    coef = coef[0:1, 0:1] * (TOK * GROUPS * C_OUT * 2.0 / (TOK * GROUPS // SAMPLES * C_OUT))
    grad_ref[...] = (coef * (direct + back[:FEAT])).astype(bf16)


class Fetched:
    def __init__(self, source, held, semaphore):
        self.held = held
        self.copy = pltpu.make_async_copy(source, held, semaphore)
        self.copy.start()

    def wait(self):
        if self.copy is not None:
            self.copy.wait()
            self.copy = None

    def __getitem__(self, index):
        self.wait()
        return self.held[index]


class Stored:
    def __init__(self, target, held, semaphore):
        self.held = held
        self.copy = pltpu.make_async_copy(held, target, semaphore)
        self.started = False

    def __setitem__(self, index, values):
        self.held[index] = values

    def start(self):
        if not self.started:
            self.copy.start()
            self.started = True

    def wait(self):
        self.copy.wait()


def call(kernel, scalars, arrays, outs, fetch=(), store=(), flops=0):
    vmem = pl.BlockSpec(memory_space=pltpu.VMEM)
    smem = pl.BlockSpec(memory_space=pltpu.SMEM)
    hbm = pl.BlockSpec(memory_space=pltpu.HBM)
    size = sum(a.size * a.dtype.itemsize for a in arrays)
    out_shape = [
        pltpu.HBM(shape, dtype) if i in store else jax.ShapeDtypeStruct(shape, dtype)
        for i, (shape, dtype) in enumerate(outs)
    ]
    arrays = [
        pltpu.with_memory_space_constraint(a, pltpu.HBM) if i in fetch else a
        for i, a in enumerate(arrays)
    ]
    moved = [arrays[i] for i in fetch] + [out_shape[i] for i in store]
    scratch = [pltpu.VMEM(a.shape, a.dtype) for a in moved]
    if moved:
        scratch.append(pltpu.SemaphoreType.DMA((len(moved),)))

    def body(*refs):
        refs = list(refs)
        at_in = len(scalars)
        at_out = at_in + len(arrays)
        at_held = at_out + len(outs)
        fetched, stored = [], []
        for n, i in enumerate(fetch):
            fetched.append(Fetched(refs[at_in + i], refs[at_held + n], refs[-1].at[n]))
            refs[at_in + i] = fetched[-1]
        for n, i in enumerate(store, len(fetch)):
            stored.append(Stored(refs[at_out + i], refs[at_held + n], refs[-1].at[n]))
            refs[at_out + i] = stored[-1]
        kernel(*refs[:at_held])
        for item in stored:
            item.start()
        for item in fetched + stored:
            item.wait()

    return pl.pallas_call(
        body,
        out_shape=out_shape,
        in_specs=[smem] * len(scalars)
        + [hbm if i in fetch else vmem for i in range(len(arrays))],
        out_specs=[hbm if i in store else vmem for i in range(len(outs))],
        scratch_shapes=scratch,
        compiler_params=pltpu.CompilerParams(vmem_limit_bytes=24 * 1024 * 1024),
        cost_estimate=pl.CostEstimate(flops=flops, bytes_accessed=size, transcendentals=0),
    )(*scalars, *arrays)


def swap(chunks, axis):
    return lax.all_to_all(chunks, axis, split_axis=0, concat_axis=0, tiled=True)


def local(
    tokens,
    modulation,
    routes,
    route_weights,
    w_first,
    w_second,
    head,
    targets,
    ref_err,
    pair_ids,
    timesteps,
):
    shard = lax.axis_index(FSDP)
    quarter = lax.axis_index(QUAD)
    leader = (lax.axis_index(SHARERS) == 0).astype(i32)
    my_sample = lax.axis_index("expert") * SAMPLES // GROUPS
    place = jnp.concatenate([jnp.stack([shard, quarter, leader, my_sample]).astype(i32), pair_ids])
    fraction = timesteps.astype(f32) / 1000.0
    keep_level = jnp.cos((fraction + 0.008) / 1.008 * (math.pi / 2.0)) ** 2
    levels = jnp.concatenate([ref_err, dpo_beta * keep_level])
    w_in = w_first[0].T

    with jax.named_scope("weights"):
        swap_pair = [(0, 1), (1, 0)]
        w_z = lax.ppermute(w_in, "zl", swap_pair)
        w_y = lax.ppermute(w_in, "yl", swap_pair)

    with jax.named_scope("routing"):
        sent, pick, base, block = call(
            routing_kernel,
            [place],
            [tokens.T, routes.T, route_weights.T, targets.T, head],
            [
                ((GROUPS, 16, LANES), bf16),
                ((GROUPS * CAP, TOK), bf16),
                ((SHARDS, LANES), f32),
                ((2, SHARDS, LANES), f32),
            ],
            store=(1, 3),
        )
    with jax.named_scope("dispatch"):
        arrived = swap(sent, "expert")
        half = HID // 2
        weights = [w_in, w_z, w_y]
        weights.append(lax.ppermute(w_z[:half], "yl", swap_pair))
        weights.append(lax.ppermute(w_y[half:], "zl", swap_pair))
        head_flat = jnp.pad(head.T.reshape(FEAT // 8, LANES), ((0, 1), (0, 0)))
        (parcel,) = call(
            parcel_kernel, [], [arrived, base, head_flat], [((SHARDS, ROWS, LANES), bf16)]
        )
        gathered = swap(parcel, FSDP)

    with jax.named_scope("projection"):
        gate = jnp.tile(jnp.repeat(modulation[:, 2].T, C_OUT, axis=1), (1, 2))
        proj, head_all = call(
            head_kernel,
            [],
            [gathered, gate, w_second[0]],
            [((SAMPLES, C_OUT, HID), f32), ((D, LANES), bf16)],
            fetch=(2,),
            store=(0, 1),
        )
        proj = swap(proj, QUAD)

    with jax.named_scope("first_layer"):
        mod = lax.dynamic_index_in_dim(modulation, quarter, 0, keepdims=False)
        act, slope, rows = call(
            first_kernel,
            [],
            [gathered, mod] + weights,
            [((4, LANES, HID), bf16), ((4, LANES, HID), f32), ((LANES, D), bf16)],
            fetch=(2, 3, 4, 5, 6),
            store=(0, 1, 2),
            flops=8 * D * HID * LANES,
        )

    with jax.named_scope("predict"):
        (part,) = call(
            predict_kernel, [place], [act, proj], [((8, C_OUT, LANES), f32)], fetch=(0,)
        )
        parts = swap(part, SHARERS)
        own, shared = call(
            own_kernel, [], [parts], [((C_OUT, LANES), f32), ((GROUPS, C_OUT, LANES), bf16)],
            store=(0,),
        )
        base_rows, facts = call(
            base_kernel, [], [gathered, rows, head_all], [((C_OUT, LANES), f32), ((72, LANES), f32)],
            fetch=(1, 2),
            store=(0, 1),
        )
        shared = swap(shared, "expert")

    with jax.named_scope("backward"):
        (parcel,) = call(
            backward_kernel,
            [place],
            [shared, own, base_rows, facts, block, proj, slope, mod, head_all, rows]
            + weights,
            [((SHARDS, PACK, LANES), bf16)],
            fetch=tuple(range(1, 15)),
            flops=8 * D * HID * LANES,
        )
        parcel = swap(parcel, FSDP)
        home, lost = call(
            mid_kernel, [], [parcel], [((GROUPS, 16, LANES), bf16), ((2, SHARDS, LANES), f32)],
            store=(1,),
        )
        home = swap(home, "expert")

    with jax.named_scope("finish"):
        grad_tokens, loss = call(
            end_kernel,
            [place, levels],
            [home, pick, lost, head],
            [((FEAT, TOK), bf16), ((1, 1), f32)],
            fetch=(1, 2),
        )
    return (grad_tokens.T, loss.reshape(()))


def solution(mesh):
    mesh = Mesh(mesh.devices.reshape(2, 2, 4, 2, 16), FSDP + ("expert",))
    in_specs = (
        P("expert", FSDP),
        P(),
        P("expert", None),
        P("expert", None),
        P("expert", None, FSDP),
        P("expert", FSDP, None),
        P(None, FSDP),
        P("expert", None),
        P(),
        P(),
        P(),
    )
    out_specs = (P("expert", FSDP), P())
    return jax.shard_map(local, mesh=mesh, in_specs=in_specs, out_specs=out_specs, check_vma=False)
```

```python
import functools
import math

import jax
import jax.numpy as jnp
from jax import lax
from jax.experimental import pallas as pl
from jax.experimental.pallas import tpu as pltpu
from jax.sharding import Mesh, PartitionSpec as P

D = 1792
TOPK = 2
C_OUT = 16
SAMPLES = 4
LANES = 128
FEAT = 56
SHARDS = 32
GROUPS = 16
CAP = 32
TOK = 256
HID = 224
PACK = 64
ROWS = 72
FSDP = ("y", "zh", "zl")
RING = ("zh", "zl")
SHARERS = ("y", "zh")


norm_eps = 1e-06
dpo_beta = 2.0
bf16 = jnp.bfloat16
f32 = jnp.float32
i32 = jnp.int32
highest = lax.Precision.HIGHEST
contract_last = (((1,), (1,)), ((), ()))
contract_first = (((0,), (0,)), ((), ()))


def dot(a, b, **kw):
    return jnp.dot(a, b, preferred_element_type=f32, **kw)


def dot_nt(a, b, **kw):
    return lax.dot_general(a, b, contract_last, preferred_element_type=f32, **kw)


def iota(shape, axis):
    return lax.broadcasted_iota(i32, shape, axis)


def high_low(values):
    high = values.astype(bf16).astype(f32)
    return high, values - high


def whole(weight):
    if isinstance(weight, tuple):
        return jnp.concatenate([part[...] for part in weight], axis=0)
    return weight[...]


def lane_blocks(tiles):
    block = iota(tiles[0].shape, 1) // CAP
    out = []
    for b in range(4):
        total = None
        for j in range(4):
            moved = tiles[j] if j == b else pltpu.roll(tiles[j], (CAP * (j - b)) % LANES, axis=1)
            total = moved if total is None else jnp.where(block == j, moved, total)
        out.append(total)
    return out


def routing_kernel(
    place_ref, tokens_ref, routes_ref, weights_ref, targets_ref, head_ref,
    sent_ref, pick_ref, base_ref, facts_ref,
):
    shard = place_ref[0]
    tokens = tokens_ref[...]
    expert = iota((GROUPS, TOK), 0)
    hits = [(routes_ref[k : k + 1, :] == expert).astype(f32) for k in range(TOPK)]
    below = (iota((TOK, TOK), 0) < iota((TOK, TOK), 1)).astype(bf16)
    earlier = dot((hits[0] + hits[1]).astype(bf16), below)
    slots = [jnp.sum(earlier * hit, axis=0, keepdims=True) for hit in hits]
    kept = [(slot < CAP).astype(f32) for slot in slots]
    lane = iota((GROUPS * CAP, TOK), 0)
    places = []
    for k in range(TOPK):
        dest = jnp.where(
            kept[k] > 0.5, routes_ref[k : k + 1, :] * CAP + slots[k].astype(i32), -1
        )
        places.append((lane == dest).astype(f32))
    pick_ref[...] = (places[0] + places[1]).astype(bf16)
    pick_ref.start()

    target_high, target_low = high_low(targets_ref[...])
    row = iota((PACK, LANES), 0)
    column = iota((PACK, LANES), 1)
    pick_fact = (row >= FEAT) & (row < FEAT + 2) & (column == 2 * shard + row - FEAT)
    pick_fact = pick_fact.astype(bf16)
    body = jnp.concatenate([tokens.astype(f32), jnp.zeros((PACK - FEAT, TOK), f32)], axis=0)
    packed = None
    for k in range(TOPK):
        other = 1 - k
        own = high_low(weights_ref[k : k + 1, :])
        partner = high_low(weights_ref[other : other + 1, :] * kept[other])
        first = jnp.ones((1, TOK), f32) if k == 0 else 1.0 - kept[0]
        facts = [
            own[0], own[1], partner[0], partner[1],
            routes_ref[other : other + 1, :].astype(f32) * kept[other],
            slots[other] * kept[other],
            first,
        ]
        line = iota((8, TOK), 0)
        table = jnp.zeros((8, TOK), f32)
        for place, fact in enumerate(facts):
            table = jnp.where(line == place, fact, table)
        table = jnp.concatenate(
            [target_high, target_low, table, jnp.zeros((LANES - 40, TOK), f32)], axis=0
        )
        features = body + dot(pick_fact, table.astype(bf16))
        part = dot_nt(features.astype(bf16), places[k].astype(bf16))
        packed = part if packed is None else packed + part
    for tile in range(4):
        pieces = [
            packed[16 * j : 16 * j + 16, tile * LANES : (tile + 1) * LANES] for j in range(4)
        ]
        for b, piece in enumerate(lane_blocks(pieces)):
            sent_ref[4 * tile + b] = piece.astype(bf16)

    base = dot(head_ref[...], tokens)
    lost = (1.0 - kept[0]) * (1.0 - kept[1])
    lost = jnp.broadcast_to(lost, (C_OUT, TOK))
    stack = jnp.concatenate([base, targets_ref[...], lost], axis=0).T
    stack = jnp.concatenate([stack, jnp.zeros((TOK, LANES - 3 * C_OUT), f32)], axis=1)
    group = iota((SHARDS, LANES), 1) // C_OUT
    for place in range(3):
        total = jnp.zeros((SHARDS, LANES), f32)
        for j in range(8):
            piece = stack[SHARDS * j : SHARDS * (j + 1)]
            shift = (C_OUT * (j - place)) % LANES
            piece = pltpu.roll(piece, shift, axis=1) if shift else piece
            total = jnp.where(group == j, piece, total)
        if place == 0:
            base_ref[...] = total
        else:
            facts_ref[place - 1] = total


def parcel_kernel(arrived_ref, base_ref, head_ref, parcel_ref):
    base_high, base_low = high_low(base_ref[...])
    row = iota((8, LANES), 0)
    head = head_ref[...].astype(f32)
    for q in range(4):
        tiles = lane_blocks([arrived_ref[4 * q + b].astype(f32) for b in range(4)])
        body = jnp.concatenate([tiles[0], tiles[1], tiles[2], tiles[3][:8]], axis=0)
        last = tiles[3][8:]
        for high in range(8):
            f = 4 * high + q
            tail = jnp.where(row == 2, base_high[f : f + 1], last)
            tail = jnp.where(row == 3, base_low[f : f + 1], tail)
            parcel_ref[f] = jnp.concatenate([body, tail, head], axis=0).astype(bf16)


def head_kernel(gathered_ref, gate_ref, w_out_ref, proj_ref, head_ref):
    pieces = []
    for f in range(SHARDS):
        rows = gathered_ref[f, PACK:ROWS].astype(f32)
        for i in range(FEAT // 8):
            pieces.append(jnp.broadcast_to(rows[i : i + 1], (8, LANES)))
    spread = jnp.concatenate(pieces, axis=0)
    lane = iota((D, LANES), 1)
    spread = jnp.where(lane // C_OUT == iota((D, LANES), 0) % 8, spread, 0.0).astype(bf16)
    fold = iota((LANES, LANES), 0) % C_OUT == iota((LANES, LANES), 1) % C_OUT
    head = dot(spread, fold.astype(bf16))
    head_ref[...] = head.astype(bf16)
    head_ref.start()
    high, low = high_low(head * gate_ref[...])
    pair = jnp.where(lane < PACK, high, low).astype(bf16)
    proj = dot(w_out_ref[...], pair)
    proj = proj + pltpu.roll(proj, PACK, axis=1)
    proj = proj.T
    for z in range(8):
        q = z % SAMPLES
        proj_ref[z] = proj[C_OUT * q : C_OUT * (q + 1)].astype(bf16)


def first_kernel(
    gathered_ref, mod_ref, w0_ref, w1_ref, w2_ref, w3_ref, w4_ref, act_ref, slope_ref, rows_ref
):
    rows = jnp.concatenate([gathered_ref[f, :FEAT].astype(f32) for f in range(SHARDS)], axis=0).T
    rows_ref[...] = rows.astype(bf16)
    rows_ref.start()
    rms = lax.rsqrt(jnp.sum(rows * rows, axis=1, keepdims=True) / D + norm_eps)
    normed = (rows * rms) * (1.0 + mod_ref[1:2, :]) + mod_ref[0:1, :]
    normed = normed.astype(bf16)
    weights = [w0_ref, w1_ref, w2_ref, (w3_ref, w4_ref)]
    for b, weight in enumerate(weights):
        pre = dot_nt(normed, whole(weight))
        cubic = math.sqrt(2.0 / math.pi)
        square = pre * pre
        tanh = jnp.tanh(cubic * (pre + 0.044715 * square * pre))
        half = 0.5 * (1.0 + tanh)
        act_ref[b] = (pre * half).astype(bf16)
        slope_ref[b] = half + 0.5 * pre * (1.0 - tanh * tanh) * (
            cubic * (1.0 + 3.0 * 0.044715 * square)
        )
        slope_ref.start(b)


def held_projections(proj_ref, z):
    lane = iota((C_OUT, HID), 1)
    after, before = proj_ref[(z + 2) % 8].astype(f32), proj_ref[(z + 6) % 8].astype(f32)
    ends = jnp.where(lane < HID // 2, after, before).astype(bf16)
    return [proj_ref[z], proj_ref[(z + 7) % 8], proj_ref[(z + 1) % 8], ends]


def predict_kernel(place_ref, act_ref, proj_ref, part_ref):
    total = None
    for b, proj in enumerate(held_projections(proj_ref, place_ref[4])):
        part = dot_nt(proj, act_ref[b])
        total = part if total is None else total + part
    for other in range(8):
        part_ref[other] = total


def own_kernel(parts_ref, shared_ref):
    own = jnp.sum(parts_ref[...], axis=0).astype(bf16)
    for e in range(GROUPS):
        shared_ref[e] = own


def base_kernel(gathered_ref, rows_ref, head_ref, base_ref, facts_ref):
    base = dot(rows_ref[...], head_ref[...]).T
    base_ref[...] = base[:C_OUT]
    tails = [gathered_ref[f, FEAT:PACK].astype(f32) for f in range(SHARDS)]
    facts = jnp.concatenate([tail[:2] for tail in tails], axis=0)
    facts_ref[:PACK] = facts
    facts_ref[PACK:] = functools.reduce(jnp.add, tails)


def backward_kernel(
    place_ref, shared_ref, base_ref, facts_ref, block_ref, proj_ref, slope_ref,
    mod_ref, head_ref, rows_ref, w0_ref, w1_ref, w2_ref, w3_ref, w4_ref, parcel_ref,
):
    shard, quarter, leader, sample = place_ref[0], place_ref[1], place_ref[2], place_ref[3]
    facts = facts_ref[...]
    target = facts[:C_OUT] + facts[C_OUT : 2 * C_OUT]
    own_w = facts[32:33] + facts[33:34]
    other_w = facts[34:35] + facts[35:36]
    first = facts[38:39]
    lane = iota((1, LANES), 1)
    source = facts[36:37].astype(i32) * LANES + facts[37:38].astype(i32) + lane // CAP * CAP
    chosen = (iota((GROUPS * LANES, LANES), 0) == source).astype(f32).astype(bf16)
    everyone = jnp.concatenate([shared_ref[e] for e in range(GROUPS)], axis=1)
    partner = dot(everyone, chosen)
    residue = base_ref[...] + own_w * shared_ref[place_ref[5]].astype(f32) + other_w * partner - target
    kept_err = jnp.sum(first * residue * residue, keepdims=True)

    lost_base = facts[PACK + 2 : PACK + 3] + facts[PACK + 3 : PACK + 4]
    lost = (lost_base - block_ref[0, pl.ds(shard, 1), :]) * block_ref[1, pl.ds(shard, 1), :]
    lost_err = jnp.sum(lost * lost, keepdims=True)
    err = jnp.where((lane == quarter) & (leader == 1), kept_err, 0.0)
    err = err + jnp.where(lane == sample, lost_err, 0.0)
    row = iota((8, LANES), 0)
    tail = jnp.zeros((8, LANES), f32)
    for place, values in enumerate(high_low(lost) + high_low(err)):
        tail = jnp.where(row == place, values, tail)

    upstream = jnp.concatenate(high_low((own_w * residue).T), axis=1).astype(bf16)
    weights = [w0_ref, w1_ref, w2_ref, (w3_ref, w4_ref)]
    total = None
    for b, proj in enumerate(held_projections(proj_ref, place_ref[4])):
        grad = slope_ref[b] * dot(upstream, jnp.concatenate([proj, proj], axis=0))
        part = dot(grad.astype(bf16), whole(weights[b]))
        total = part if total is None else total + part
    rows = rows_ref[...].astype(f32)
    rms = lax.rsqrt(jnp.sum(rows * rows, axis=1, keepdims=True) / D + norm_eps)
    total = total * (rms * (1.0 + mod_ref[1:2, :]))
    inner = jnp.sum(total * rows, axis=1, keepdims=True) * (rms * rms / D)
    high, low = high_low(first * residue * 0.125)
    direct = jnp.concatenate([high, low, jnp.zeros((LANES - 2 * C_OUT, LANES), f32)], axis=0)
    total = total - rows * inner + dot_nt(direct.T.astype(bf16), head_ref[...])
    total = total.T
    for f in range(SHARDS):
        parcel_ref[f] = jnp.concatenate(
            [total[FEAT * f : FEAT * (f + 1)], tail], axis=0
        ).astype(bf16)


def mid_kernel(parcel_ref, home_ref, lost_ref):
    lane = iota((1, LANES), 1)
    row = iota((8, LANES), 0)
    sums, tails = [], []
    for q in range(4):
        total = None
        for high in range(8):
            f = 4 * high + q
            part = parcel_ref[f].astype(f32)
            lost_ref[0, f : f + 1] = part[FEAT : FEAT + 1]
            lost_ref[1, f : f + 1] = part[FEAT + 1 : FEAT + 2]
            total = part if total is None else total + part
        sums.append(total[:FEAT])
        tails.append(total[FEAT:])
    tail = tails[0] + tails[1] + tails[2] + tails[3]
    err = jnp.where(lane < SAMPLES, tail[2:3] + tail[3:4], 0.0)
    err = err + pltpu.roll(err, CAP, axis=1)
    err = err + pltpu.roll(err, 2 * CAP, axis=1)
    high, low = high_low(err)
    tail = jnp.where(row == 0, high, 0.0) + jnp.where(row == 1, low, 0.0)
    for q in range(4):
        full = jnp.concatenate([sums[q], tail], axis=0)
        tiles = lane_blocks([full[16 * j : 16 * j + 16] for j in range(4)])
        for b in range(4):
            home_ref[4 * q + b] = tiles[b].astype(bf16)


def end_kernel(
    place_ref, levels_ref, home_ref, pick_ref, lost_ref, head_ref,
    grad_ref, loss_ref,
):
    sample = place_ref[3].astype(f32)
    pairs = [levels_ref[SAMPLES + 2 + i] for i in range(SAMPLES)]
    columns = []
    for tile in range(4):
        tiles = lane_blocks([home_ref[4 * tile + b].astype(f32) for b in range(4)])
        columns.append(jnp.concatenate(tiles, axis=0))
    home = jnp.concatenate(columns, axis=1)
    back = dot(home.astype(bf16), pick_ref[...])
    err = functools.reduce(jnp.add, [column[FEAT : FEAT + 1] for column in columns])
    err = err + functools.reduce(jnp.add, [column[FEAT + 1 : FEAT + 2] for column in columns])
    err = jnp.broadcast_to(err, (8, LANES)) / (TOK * GROUPS // SAMPLES * C_OUT)
    lane = iota((8, LANES), 1) % CAP
    excess = []
    for s in range(SAMPLES):
        total = jnp.sum(jnp.where(lane == s, err, 0.0), axis=1, keepdims=True)
        excess.append(jnp.broadcast_to(total, (8, LANES)) - levels_ref[s])
    loss, coef = 0.0, 0.0
    for k in range(2):
        winner, loser = pairs[2 * k], pairs[2 * k + 1]
        margin = 0.0
        for s in range(SAMPLES):
            margin = margin + jnp.where(winner == s, excess[s], 0.0)
        for s in range(SAMPLES):
            margin = margin - jnp.where(loser == s, excess[s], 0.0)
        down = levels_ref[SAMPLES + k] * margin
        loss = loss + jnp.maximum(down, 0.0) + jnp.log1p(jnp.exp(-jnp.abs(down)))
        rate = levels_ref[SAMPLES + k] / (1.0 + jnp.exp(-down)) * 0.5
        coef = coef + jnp.where(winner == sample, rate, 0.0)
        coef = coef - jnp.where(loser == sample, rate, 0.0)
    loss_ref[...] = loss[0:1, 0:1] * 0.5
    lane = iota((SHARDS, LANES), 1) // C_OUT
    head_tile = jnp.concatenate([head_ref[...]] * 8, axis=0).astype(f32).T.astype(bf16)
    direct = 0.0
    for part in range(2):
        lost = [jnp.where(lane == j, lost_ref[part], 0.0) for j in range(8)]
        direct = direct + dot_nt(head_tile, jnp.concatenate(lost, axis=0).astype(bf16))
    coef = coef[0:1, 0:1] * (TOK * GROUPS * C_OUT * 2.0 / (TOK * GROUPS // SAMPLES * C_OUT))
    grad_ref[...] = (coef * (direct + back[:FEAT])).astype(bf16)


class Fetched:
    def __init__(self, source, held, semaphore):
        self.held = held
        self.copy = pltpu.make_async_copy(source, held, semaphore)
        self.copy.start()

    def wait(self):
        if self.copy is not None:
            self.copy.wait()
            self.copy = None

    def __getitem__(self, index):
        self.wait()
        return self.held[index]


class Stored:
    def __init__(self, target, held, semaphore, parts):
        self.held = held
        if parts == 1:
            self.copies = [pltpu.make_async_copy(held, target, semaphore.at[0])]
        else:
            self.copies = [
                pltpu.make_async_copy(held.at[i], target.at[i], semaphore.at[i])
                for i in range(parts)
            ]
        self.started = [False] * parts

    def __setitem__(self, index, values):
        self.held[index] = values

    def start(self, part=0):
        if not self.started[part]:
            self.copies[part].start()
            self.started[part] = True

    def finish(self):
        for part in range(len(self.copies)):
            self.start(part)

    def wait(self):
        for copy in self.copies:
            copy.wait()


def call(kernel, scalars, arrays, outs, fetch=(), store=(), parts={}, flops=0):
    vmem = pl.BlockSpec(memory_space=pltpu.VMEM)
    smem = pl.BlockSpec(memory_space=pltpu.SMEM)
    hbm = pl.BlockSpec(memory_space=pltpu.HBM)
    size = sum(a.size * a.dtype.itemsize for a in arrays)
    out_shape = [
        pltpu.HBM(shape, dtype) if i in store else jax.ShapeDtypeStruct(shape, dtype)
        for i, (shape, dtype) in enumerate(outs)
    ]
    arrays = [
        pltpu.with_memory_space_constraint(a, pltpu.HBM) if i in fetch else a
        for i, a in enumerate(arrays)
    ]
    moved = [arrays[i] for i in fetch] + [out_shape[i] for i in store]
    scratch = [pltpu.VMEM(a.shape, a.dtype) for a in moved]
    counts = [1] * len(fetch) + [parts.get(i, 1) for i in store]
    starts = [sum(counts[:n]) for n in range(len(counts))]
    if moved:
        scratch.append(pltpu.SemaphoreType.DMA((sum(counts),)))

    def body(*refs):
        refs = list(refs)
        at_in = len(scalars)
        at_out = at_in + len(arrays)
        at_held = at_out + len(outs)
        fetched, stored = [], []
        for n, i in enumerate(fetch):
            fetched.append(Fetched(refs[at_in + i], refs[at_held + n], refs[-1].at[n]))
            refs[at_in + i] = fetched[-1]
        for n, i in enumerate(store, len(fetch)):
            semaphores = refs[-1].at[pl.ds(starts[n], counts[n])]
            stored.append(Stored(refs[at_out + i], refs[at_held + n], semaphores, counts[n]))
            refs[at_out + i] = stored[-1]
        kernel(*refs[:at_held])
        for item in stored:
            item.finish()
        for item in fetched + stored:
            item.wait()

    return pl.pallas_call(
        body,
        out_shape=out_shape,
        in_specs=[smem] * len(scalars)
        + [hbm if i in fetch else vmem for i in range(len(arrays))],
        out_specs=[hbm if i in store else vmem for i in range(len(outs))],
        scratch_shapes=scratch,
        compiler_params=pltpu.CompilerParams(vmem_limit_bytes=24 * 1024 * 1024),
        cost_estimate=pl.CostEstimate(flops=flops, bytes_accessed=size, transcendentals=0),
    )(*scalars, *arrays)


def swap(chunks, axis):
    return lax.all_to_all(chunks, axis, split_axis=0, concat_axis=0, tiled=True)


def local(
    tokens,
    modulation,
    routes,
    route_weights,
    w_first,
    w_second,
    head,
    targets,
    ref_err,
    pair_ids,
    timesteps,
):
    shard = lax.axis_index(FSDP)
    ring = lax.axis_index(RING)
    quarter = lax.axis_index("zl")
    leader = (lax.axis_index(SHARERS) == 0).astype(i32)
    my_sample = lax.axis_index("expert") * SAMPLES // GROUPS
    place = jnp.stack([shard, quarter, leader, my_sample, ring, lax.axis_index("expert")]).astype(i32)
    fraction = timesteps.astype(f32) / 1000.0
    keep_level = jnp.cos((fraction + 0.008) / 1.008 * (math.pi / 2.0)) ** 2
    levels = jnp.concatenate([ref_err, dpo_beta * keep_level, pair_ids.astype(f32)])
    w_in = w_first[0].T

    with jax.named_scope("weights"):
        up = [(z, (z + 1) % 8) for z in range(8)]
        down = [(z, (z + 7) % 8) for z in range(8)]
        w_before = lax.ppermute(w_in, RING, up)
        w_after = lax.ppermute(w_in, RING, down)

    with jax.named_scope("routing"):
        sent, pick, base, block = call(
            routing_kernel,
            [place],
            [tokens.T, routes.T, route_weights.T, targets.T, head],
            [
                ((GROUPS, 16, LANES), bf16),
                ((GROUPS * CAP, TOK), bf16),
                ((SHARDS, LANES), f32),
                ((2, SHARDS, LANES), f32),
            ],
            store=(1, 3),
        )
    with jax.named_scope("dispatch"):
        arrived = swap(sent, "expert")
        arrived, w_before, w_after = lax.optimization_barrier((arrived, w_before, w_after))
        half = HID // 2
        weights = [
            w_in,
            w_before,
            w_after,
            lax.ppermute(w_after[:half], RING, down),
            lax.ppermute(w_before[half:], RING, up),
        ]
        head_flat = jnp.pad(head.T.reshape(FEAT // 8, LANES), ((0, 1), (0, 0)))
        (parcel,) = call(
            parcel_kernel, [], [arrived, base, head_flat], [((SHARDS, ROWS, LANES), bf16)]
        )
        gathered = swap(parcel, FSDP)

    with jax.named_scope("projection"):
        gate = jnp.tile(jnp.repeat(modulation[:, 2].T, C_OUT, axis=1), (1, 2))
        proj, head_all = call(
            head_kernel,
            [],
            [gathered, gate, w_second[0]],
            [((8, C_OUT, HID), bf16), ((D, LANES), bf16)],
            fetch=(2,),
            store=(0, 1),
        )
        proj = swap(proj, RING)

    with jax.named_scope("first_layer"):
        mod = lax.dynamic_index_in_dim(modulation, quarter, 0, keepdims=False)
        act, slope, rows = call(
            first_kernel,
            [],
            [gathered, mod] + weights,
            [((4, LANES, HID), bf16), ((4, LANES, HID), f32), ((LANES, D), bf16)],
            fetch=(2, 3, 4),
            store=(1, 2),
            parts={1: 4},
            flops=8 * D * HID * LANES,
        )

    with jax.named_scope("predict"):
        (part,) = call(
            predict_kernel, [place], [act, proj], [((8, C_OUT, LANES), f32)]
        )
        parts = swap(part, SHARERS)
        (shared,) = call(own_kernel, [], [parts], [((GROUPS, C_OUT, LANES), bf16)])
        base_rows, facts = call(
            base_kernel, [], [gathered, rows, head_all], [((C_OUT, LANES), f32), ((72, LANES), f32)],
            fetch=(1, 2),
            store=(0, 1),
        )
        shared = swap(shared, "expert")

    with jax.named_scope("backward"):
        (parcel,) = call(
            backward_kernel,
            [place],
            [shared, base_rows, facts, block, proj, slope, mod, head_all, rows]
            + weights,
            [((SHARDS, PACK, LANES), bf16)],
            fetch=(1, 2, 3, 4, 5, 9, 10, 11, 12, 13, 6, 7, 8),
            flops=8 * D * HID * LANES,
        )
        parcel = swap(parcel, FSDP)
        home, lost = call(
            mid_kernel, [], [parcel], [((GROUPS, 16, LANES), bf16), ((2, SHARDS, LANES), f32)],
            store=(1,),
        )
        home = swap(home, "expert")

    with jax.named_scope("finish"):
        grad_tokens, loss = call(
            end_kernel,
            [place, levels],
            [home, pick, lost, head],
            [((FEAT, TOK), bf16), ((1, 1), f32)],
            fetch=(1, 2),
        )
    return (grad_tokens.T, loss.reshape(()))


def solution(mesh):
    mesh = Mesh(mesh.devices.reshape(4, 2, 4, 16), FSDP + ("expert",))
    in_specs = (
        P("expert", FSDP),
        P(),
        P("expert", None),
        P("expert", None),
        P("expert", None, FSDP),
        P("expert", FSDP, None),
        P(None, FSDP),
        P("expert", None),
        P(),
        P(),
        P(),
    )
    out_specs = (P("expert", FSDP), P())
    return jax.shard_map(local, mesh=mesh, in_specs=in_specs, out_specs=out_specs, check_vma=False)
```

```python
import functools
import math

import jax
import jax.numpy as jnp
from jax import lax
from jax.experimental import pallas as pl
from jax.experimental.pallas import tpu as pltpu
from jax.sharding import Mesh, PartitionSpec as P

D = 1792
TOPK = 2
C_OUT = 16
SAMPLES = 4
LANES = 128
FEAT = 56
SHARDS = 32
GROUPS = 16
CAP = 32
TOK = 256
HID = 224
PACK = 64
ROWS = 72
FSDP = ("y", "zh", "zl")
RING = ("zh", "zl")
SHARERS = ("y", "zh")


norm_eps = 1e-06
dpo_beta = 2.0
bf16 = jnp.bfloat16
f32 = jnp.float32
i32 = jnp.int32
highest = lax.Precision.HIGHEST
contract_last = (((1,), (1,)), ((), ()))
contract_first = (((0,), (0,)), ((), ()))


def dot(a, b, **kw):
    return jnp.dot(a, b, preferred_element_type=f32, **kw)


def dot_nt(a, b, **kw):
    return lax.dot_general(a, b, contract_last, preferred_element_type=f32, **kw)


def iota(shape, axis):
    return lax.broadcasted_iota(i32, shape, axis)


def high_low(values):
    high = values.astype(bf16).astype(f32)
    return high, values - high


def whole(weight):
    if isinstance(weight, tuple):
        return jnp.concatenate([part[...] for part in weight], axis=0)
    return weight[...]


def lane_blocks(tiles):
    block = iota(tiles[0].shape, 1) // CAP
    out = []
    for b in range(4):
        total = None
        for j in range(4):
            moved = tiles[j] if j == b else pltpu.roll(tiles[j], (CAP * (j - b)) % LANES, axis=1)
            total = moved if total is None else jnp.where(block == j, moved, total)
        out.append(total)
    return out


def routing_kernel(
    place_ref, tokens_ref, routes_ref, weights_ref, targets_ref, head_ref,
    sent_ref, pick_ref, base_ref, facts_ref,
):
    shard = place_ref[0]
    tokens = tokens_ref[...]
    expert = iota((GROUPS, TOK), 0)
    hits = [(routes_ref[k : k + 1, :] == expert).astype(f32) for k in range(TOPK)]
    below = (iota((TOK, TOK), 0) < iota((TOK, TOK), 1)).astype(bf16)
    earlier = dot((hits[0] + hits[1]).astype(bf16), below)
    slots = [jnp.sum(earlier * hit, axis=0, keepdims=True) for hit in hits]
    kept = [(slot < CAP).astype(f32) for slot in slots]
    lane = iota((GROUPS * CAP, TOK), 0)
    places = []
    for k in range(TOPK):
        dest = jnp.where(
            kept[k] > 0.5, routes_ref[k : k + 1, :] * CAP + slots[k].astype(i32), -1
        )
        places.append((lane == dest).astype(f32))
    pick_ref[...] = (places[0] + places[1]).astype(bf16)
    pick_ref.start()

    target_high, target_low = high_low(targets_ref[...])
    row = iota((PACK, LANES), 0)
    column = iota((PACK, LANES), 1)
    pick_fact = (row >= FEAT) & (row < FEAT + 2) & (column == 2 * shard + row - FEAT)
    pick_fact = pick_fact.astype(bf16)
    body = jnp.concatenate([tokens.astype(f32), jnp.zeros((PACK - FEAT, TOK), f32)], axis=0)
    packed = None
    for k in range(TOPK):
        other = 1 - k
        own = high_low(weights_ref[k : k + 1, :])
        partner = high_low(weights_ref[other : other + 1, :] * kept[other])
        first = jnp.ones((1, TOK), f32) if k == 0 else 1.0 - kept[0]
        facts = [
            own[0], own[1], partner[0], partner[1],
            routes_ref[other : other + 1, :].astype(f32) * kept[other],
            slots[other] * kept[other],
            first,
        ]
        line = iota((8, TOK), 0)
        table = jnp.zeros((8, TOK), f32)
        for place, fact in enumerate(facts):
            table = jnp.where(line == place, fact, table)
        table = jnp.concatenate(
            [target_high, target_low, table, jnp.zeros((LANES - 40, TOK), f32)], axis=0
        )
        features = body + dot(pick_fact, table.astype(bf16))
        part = dot_nt(features.astype(bf16), places[k].astype(bf16))
        packed = part if packed is None else packed + part
    for tile in range(4):
        pieces = [
            packed[16 * j : 16 * j + 16, tile * LANES : (tile + 1) * LANES] for j in range(4)
        ]
        for b, piece in enumerate(lane_blocks(pieces)):
            sent_ref[4 * tile + b] = piece.astype(bf16)

    base = dot(head_ref[...], tokens)
    lost = (1.0 - kept[0]) * (1.0 - kept[1])
    lost = jnp.broadcast_to(lost, (C_OUT, TOK))
    stack = jnp.concatenate([base, targets_ref[...], lost], axis=0).T
    stack = jnp.concatenate([stack, jnp.zeros((TOK, LANES - 3 * C_OUT), f32)], axis=1)
    group = iota((SHARDS, LANES), 1) // C_OUT
    for place in range(3):
        total = jnp.zeros((SHARDS, LANES), f32)
        for j in range(8):
            piece = stack[SHARDS * j : SHARDS * (j + 1)]
            shift = (C_OUT * (j - place)) % LANES
            piece = pltpu.roll(piece, shift, axis=1) if shift else piece
            total = jnp.where(group == j, piece, total)
        if place == 0:
            base_ref[...] = total
        else:
            facts_ref[place - 1] = total


def parcel_kernel(arrived_ref, base_ref, head_ref, parcel_ref):
    base_high, base_low = high_low(base_ref[...])
    row = iota((8, LANES), 0)
    head = head_ref[...].astype(f32)
    for q in range(4):
        tiles = lane_blocks([arrived_ref[4 * q + b].astype(f32) for b in range(4)])
        body = jnp.concatenate([tiles[0], tiles[1], tiles[2], tiles[3][:8]], axis=0)
        last = tiles[3][8:]
        for high in range(8):
            f = 4 * high + q
            tail = jnp.where(row == 2, base_high[f : f + 1], last)
            tail = jnp.where(row == 3, base_low[f : f + 1], tail)
            parcel_ref[f] = jnp.concatenate([body, tail, head], axis=0).astype(bf16)


def head_kernel(gathered_ref, gate_ref, w_out_ref, proj_ref, head_ref):
    pieces = []
    for f in range(SHARDS):
        rows = gathered_ref[f, PACK:ROWS].astype(f32)
        for i in range(FEAT // 8):
            pieces.append(jnp.broadcast_to(rows[i : i + 1], (8, LANES)))
    spread = jnp.concatenate(pieces, axis=0)
    lane = iota((D, LANES), 1)
    spread = jnp.where(lane // C_OUT == iota((D, LANES), 0) % 8, spread, 0.0).astype(bf16)
    fold = iota((LANES, LANES), 0) % C_OUT == iota((LANES, LANES), 1) % C_OUT
    head = dot(spread, fold.astype(bf16))
    head_ref[...] = head.astype(bf16)
    head_ref.start()
    high, low = high_low(head * gate_ref[...])
    pair = jnp.where(lane < PACK, high, low).astype(bf16)
    proj = dot(w_out_ref[...], pair)
    proj = proj + pltpu.roll(proj, PACK, axis=1)
    proj = proj.T
    for z in range(8):
        q = z % SAMPLES
        proj_ref[z] = proj[C_OUT * q : C_OUT * (q + 1)].astype(bf16)


def first_kernel(
    place_ref, gathered_ref, mod_ref, w0_ref, w1_ref, w2_ref, w3_ref, w4_ref, act_ref, slope_ref, rows_ref
):
    rows = jnp.concatenate([gathered_ref[f, :FEAT].astype(f32) for f in range(SHARDS)], axis=0).T
    rows_ref[...] = rows.astype(bf16)
    rows_ref.start()
    rms = lax.rsqrt(jnp.sum(rows * rows, axis=1, keepdims=True) / D + norm_eps)
    mine = pl.ds(place_ref[1], 1)
    normed = (rows * rms) * (1.0 + mod_ref[1, mine, :]) + mod_ref[0, mine, :]
    normed = normed.astype(bf16)
    weights = [w0_ref, w1_ref, w2_ref, (w3_ref, w4_ref)]
    for b, weight in enumerate(weights):
        pre = dot_nt(normed, whole(weight))
        cubic = math.sqrt(2.0 / math.pi)
        square = pre * pre
        tanh = jnp.tanh(cubic * (pre + 0.044715 * square * pre))
        half = 0.5 * (1.0 + tanh)
        act_ref[b] = (pre * half).astype(bf16)
        slope_ref[b] = half + 0.5 * pre * (1.0 - tanh * tanh) * (
            cubic * (1.0 + 3.0 * 0.044715 * square)
        )
        slope_ref.start(b)


def held_projections(proj_ref, z):
    lane = iota((C_OUT, HID), 1)
    after, before = proj_ref[(z + 2) % 8].astype(f32), proj_ref[(z + 6) % 8].astype(f32)
    ends = jnp.where(lane < HID // 2, after, before).astype(bf16)
    return [proj_ref[z], proj_ref[(z + 7) % 8], proj_ref[(z + 1) % 8], ends]


def predict_kernel(place_ref, act_ref, proj_ref, part_ref):
    total = None
    for b, proj in enumerate(held_projections(proj_ref, place_ref[4])):
        part = dot_nt(proj, act_ref[b])
        total = part if total is None else total + part
    for other in range(8):
        part_ref[other] = total


def own_kernel(parts_ref, shared_ref):
    own = jnp.sum(parts_ref[...], axis=0).astype(bf16)
    for e in range(GROUPS):
        shared_ref[e] = own


def base_kernel(gathered_ref, rows_ref, head_ref, base_ref, facts_ref):
    base = dot(rows_ref[...], head_ref[...]).T
    base_ref[...] = base[:C_OUT]
    tails = [gathered_ref[f, FEAT:PACK].astype(f32) for f in range(SHARDS)]
    facts = jnp.concatenate([tail[:2] for tail in tails], axis=0)
    facts_ref[:PACK] = facts
    facts_ref[PACK:] = functools.reduce(jnp.add, tails)


def backward_kernel(
    place_ref, shared_ref, base_ref, facts_ref, block_ref, proj_ref, slope_ref,
    mod_ref, head_ref, rows_ref, w0_ref, w1_ref, w2_ref, w3_ref, w4_ref, parcel_ref,
):
    shard, quarter, leader, sample = place_ref[0], place_ref[1], place_ref[2], place_ref[3]
    facts = facts_ref[...]
    target = facts[:C_OUT] + facts[C_OUT : 2 * C_OUT]
    own_w = facts[32:33] + facts[33:34]
    other_w = facts[34:35] + facts[35:36]
    first = facts[38:39]
    lane = iota((1, LANES), 1)
    source = facts[36:37].astype(i32) * LANES + facts[37:38].astype(i32) + lane // CAP * CAP
    chosen = (iota((GROUPS * LANES, LANES), 0) == source).astype(f32).astype(bf16)
    everyone = jnp.concatenate([shared_ref[e] for e in range(GROUPS)], axis=1)
    partner = dot(everyone, chosen)
    residue = base_ref[...] + own_w * shared_ref[place_ref[5]].astype(f32) + other_w * partner - target
    kept_err = jnp.sum(first * residue * residue, keepdims=True)

    lost_base = facts[PACK + 2 : PACK + 3] + facts[PACK + 3 : PACK + 4]
    lost = (lost_base - block_ref[0, pl.ds(shard, 1), :]) * block_ref[1, pl.ds(shard, 1), :]
    lost_err = jnp.sum(lost * lost, keepdims=True)
    err = jnp.where((lane == quarter) & (leader == 1), kept_err, 0.0)
    err = err + jnp.where(lane == sample, lost_err, 0.0)
    row = iota((8, LANES), 0)
    tail = jnp.zeros((8, LANES), f32)
    for place, values in enumerate(high_low(lost) + high_low(err)):
        tail = jnp.where(row == place, values, tail)

    upstream = jnp.concatenate(high_low((own_w * residue).T), axis=1).astype(bf16)
    weights = [w0_ref, w1_ref, w2_ref, (w3_ref, w4_ref)]
    total = None
    for b, proj in enumerate(held_projections(proj_ref, place_ref[4])):
        grad = slope_ref[b] * dot(upstream, jnp.concatenate([proj, proj], axis=0))
        part = dot(grad.astype(bf16), whole(weights[b]))
        total = part if total is None else total + part
    rows = rows_ref[...].astype(f32)
    rms = lax.rsqrt(jnp.sum(rows * rows, axis=1, keepdims=True) / D + norm_eps)
    total = total * (rms * (1.0 + mod_ref[1, pl.ds(quarter, 1), :]))
    inner = jnp.sum(total * rows, axis=1, keepdims=True) * (rms * rms / D)
    high, low = high_low(first * residue * 0.125)
    direct = jnp.concatenate([high, low, jnp.zeros((LANES - 2 * C_OUT, LANES), f32)], axis=0)
    total = total - rows * inner + dot_nt(direct.T.astype(bf16), head_ref[...])
    total = total.T
    for f in range(SHARDS):
        parcel_ref[f] = jnp.concatenate(
            [total[FEAT * f : FEAT * (f + 1)], tail], axis=0
        ).astype(bf16)


def mid_kernel(parcel_ref, home_ref):
    lane = iota((1, LANES), 1)
    row = iota((8, LANES), 0)
    sums, tails = [], []
    for q in range(4):
        total = None
        for high in range(8):
            f = 4 * high + q
            part = parcel_ref[f].astype(f32)
            total = part if total is None else total + part
        sums.append(total[:FEAT])
        tails.append(total[FEAT:])
    tail = tails[0] + tails[1] + tails[2] + tails[3]
    err = jnp.where(lane < SAMPLES, tail[2:3] + tail[3:4], 0.0)
    err = err + pltpu.roll(err, CAP, axis=1)
    err = err + pltpu.roll(err, 2 * CAP, axis=1)
    high, low = high_low(err)
    tail = jnp.where(row == 0, high, 0.0) + jnp.where(row == 1, low, 0.0)
    for q in range(4):
        full = jnp.concatenate([sums[q], tail], axis=0)
        tiles = lane_blocks([full[16 * j : 16 * j + 16] for j in range(4)])
        for b in range(4):
            home_ref[4 * q + b] = tiles[b].astype(bf16)


def direct_kernel(parcel_ref, head_ref, direct_ref):
    tails = [parcel_ref[f, FEAT:].astype(f32) for f in range(SHARDS)]
    lane = iota((SHARDS, LANES), 1) // C_OUT
    head_tile = jnp.concatenate([head_ref[...]] * 8, axis=0).astype(f32).T.astype(bf16)
    direct = 0.0
    for part in range(2):
        rows = jnp.concatenate([tail[part : part + 1] for tail in tails], axis=0)
        lost = [jnp.where(lane == j, rows, 0.0) for j in range(8)]
        direct = direct + dot_nt(head_tile, jnp.concatenate(lost, axis=0).astype(bf16))
    direct_ref[...] = direct


def end_kernel(
    place_ref, levels_ref, home_ref, pick_ref, direct_ref,
    grad_ref, loss_ref,
):
    sample = place_ref[3].astype(f32)
    pairs = [levels_ref[SAMPLES + 2 + i] for i in range(SAMPLES)]
    columns = []
    for tile in range(4):
        tiles = lane_blocks([home_ref[4 * tile + b].astype(f32) for b in range(4)])
        columns.append(jnp.concatenate(tiles, axis=0))
    home = jnp.concatenate(columns, axis=1)
    back = dot(home.astype(bf16), pick_ref[...])
    err = functools.reduce(jnp.add, [column[FEAT : FEAT + 1] for column in columns])
    err = err + functools.reduce(jnp.add, [column[FEAT + 1 : FEAT + 2] for column in columns])
    err = jnp.broadcast_to(err, (8, LANES)) / (TOK * GROUPS // SAMPLES * C_OUT)
    lane = iota((8, LANES), 1) % CAP
    excess = []
    for s in range(SAMPLES):
        total = jnp.sum(jnp.where(lane == s, err, 0.0), axis=1, keepdims=True)
        excess.append(jnp.broadcast_to(total, (8, LANES)) - levels_ref[s])
    loss, coef = 0.0, 0.0
    for k in range(2):
        winner, loser = pairs[2 * k], pairs[2 * k + 1]
        margin = 0.0
        for s in range(SAMPLES):
            margin = margin + jnp.where(winner == s, excess[s], 0.0)
        for s in range(SAMPLES):
            margin = margin - jnp.where(loser == s, excess[s], 0.0)
        down = levels_ref[SAMPLES + k] * margin
        loss = loss + jnp.maximum(down, 0.0) + jnp.log1p(jnp.exp(-jnp.abs(down)))
        rate = levels_ref[SAMPLES + k] / (1.0 + jnp.exp(-down)) * 0.5
        coef = coef + jnp.where(winner == sample, rate, 0.0)
        coef = coef - jnp.where(loser == sample, rate, 0.0)
    loss_ref[...] = loss[0:1, 0:1] * 0.5
    coef = coef[0:1, 0:1] * (TOK * GROUPS * C_OUT * 2.0 / (TOK * GROUPS // SAMPLES * C_OUT))
    grad_ref[...] = (coef * (direct_ref[...] + back[:FEAT])).astype(bf16)


class Fetched:
    def __init__(self, source, held, semaphore):
        self.held = held
        self.copy = pltpu.make_async_copy(source, held, semaphore)
        self.copy.start()

    def wait(self):
        if self.copy is not None:
            self.copy.wait()
            self.copy = None

    def __getitem__(self, index):
        self.wait()
        return self.held[index]


class Stored:
    def __init__(self, target, held, semaphore, parts):
        self.held = held
        if parts == 1:
            self.copies = [pltpu.make_async_copy(held, target, semaphore.at[0])]
        else:
            self.copies = [
                pltpu.make_async_copy(held.at[i], target.at[i], semaphore.at[i])
                for i in range(parts)
            ]
        self.started = [False] * parts

    def __setitem__(self, index, values):
        self.held[index] = values

    def start(self, part=0):
        if not self.started[part]:
            self.copies[part].start()
            self.started[part] = True

    def finish(self):
        for part in range(len(self.copies)):
            self.start(part)

    def wait(self):
        for copy in self.copies:
            copy.wait()


def call(kernel, scalars, arrays, outs, fetch=(), store=(), parts={}, flops=0):
    vmem = pl.BlockSpec(memory_space=pltpu.VMEM)
    smem = pl.BlockSpec(memory_space=pltpu.SMEM)
    hbm = pl.BlockSpec(memory_space=pltpu.HBM)
    size = sum(a.size * a.dtype.itemsize for a in arrays)
    out_shape = [
        pltpu.HBM(shape, dtype) if i in store else jax.ShapeDtypeStruct(shape, dtype)
        for i, (shape, dtype) in enumerate(outs)
    ]
    arrays = [
        pltpu.with_memory_space_constraint(a, pltpu.HBM) if i in fetch else a
        for i, a in enumerate(arrays)
    ]
    moved = [arrays[i] for i in fetch] + [out_shape[i] for i in store]
    scratch = [pltpu.VMEM(a.shape, a.dtype) for a in moved]
    counts = [1] * len(fetch) + [parts.get(i, 1) for i in store]
    starts = [sum(counts[:n]) for n in range(len(counts))]
    if moved:
        scratch.append(pltpu.SemaphoreType.DMA((sum(counts),)))

    def body(*refs):
        refs = list(refs)
        at_in = len(scalars)
        at_out = at_in + len(arrays)
        at_held = at_out + len(outs)
        fetched, stored = [], []
        for n, i in enumerate(fetch):
            fetched.append(Fetched(refs[at_in + i], refs[at_held + n], refs[-1].at[n]))
            refs[at_in + i] = fetched[-1]
        for n, i in enumerate(store, len(fetch)):
            semaphores = refs[-1].at[pl.ds(starts[n], counts[n])]
            stored.append(Stored(refs[at_out + i], refs[at_held + n], semaphores, counts[n]))
            refs[at_out + i] = stored[-1]
        kernel(*refs[:at_held])
        for item in stored:
            item.finish()
        for item in fetched + stored:
            item.wait()

    return pl.pallas_call(
        body,
        out_shape=out_shape,
        in_specs=[smem] * len(scalars)
        + [hbm if i in fetch else vmem for i in range(len(arrays))],
        out_specs=[hbm if i in store else vmem for i in range(len(outs))],
        scratch_shapes=scratch,
        compiler_params=pltpu.CompilerParams(vmem_limit_bytes=24 * 1024 * 1024),
        cost_estimate=pl.CostEstimate(flops=flops, bytes_accessed=size, transcendentals=0),
    )(*scalars, *arrays)


def swap(chunks, axis):
    return lax.all_to_all(chunks, axis, split_axis=0, concat_axis=0, tiled=True)


def local(
    tokens,
    modulation,
    routes,
    route_weights,
    w_first,
    w_second,
    head,
    targets,
    ref_err,
    pair_ids,
    timesteps,
):
    shard = lax.axis_index(FSDP)
    ring = lax.axis_index(RING)
    quarter = lax.axis_index("zl")
    leader = (lax.axis_index(SHARERS) == 0).astype(i32)
    my_sample = lax.axis_index("expert") * SAMPLES // GROUPS
    place = jnp.stack([shard, quarter, leader, my_sample, ring, lax.axis_index("expert")]).astype(i32)
    fraction = timesteps.astype(f32) / 1000.0
    keep_level = jnp.cos((fraction + 0.008) / 1.008 * (math.pi / 2.0)) ** 2
    levels = jnp.concatenate([ref_err, dpo_beta * keep_level, pair_ids.astype(f32)])
    w_in = w_first[0].T
    mod = modulation.transpose(1, 0, 2)

    with jax.named_scope("weights"):
        up = [(z, (z + 1) % 8) for z in range(8)]
        down = [(z, (z + 7) % 8) for z in range(8)]
        w_before = lax.ppermute(w_in, RING, up)
        w_after = lax.ppermute(w_in, RING, down)

    with jax.named_scope("routing"):
        sent, pick, base, block = call(
            routing_kernel,
            [place],
            [tokens.T, routes.T, route_weights.T, targets.T, head],
            [
                ((GROUPS, 16, LANES), bf16),
                ((GROUPS * CAP, TOK), bf16),
                ((SHARDS, LANES), f32),
                ((2, SHARDS, LANES), f32),
            ],
            store=(1, 3),
        )
    with jax.named_scope("dispatch"):
        arrived = swap(sent, "expert")
        arrived, w_before, w_after = lax.optimization_barrier((arrived, w_before, w_after))
        half = HID // 2
        weights = [
            w_in,
            w_before,
            w_after,
            lax.ppermute(w_after[:half], RING, down),
            lax.ppermute(w_before[half:], RING, up),
        ]
        head_flat = jnp.pad(head.T.reshape(FEAT // 8, LANES), ((0, 1), (0, 0)))
        (parcel,) = call(
            parcel_kernel, [], [arrived, base, head_flat], [((SHARDS, ROWS, LANES), bf16)]
        )
        gathered = swap(parcel, FSDP)

    with jax.named_scope("projection"):
        gate = jnp.tile(jnp.repeat(mod[2].T, C_OUT, axis=1), (1, 2))
        proj, head_all = call(
            head_kernel,
            [],
            [gathered, gate, w_second[0]],
            [((8, C_OUT, HID), bf16), ((D, LANES), bf16)],
            store=(0, 1),
        )
        proj = swap(proj, RING)

    with jax.named_scope("first_layer"):
        act, slope, rows = call(
            first_kernel,
            [place],
            [gathered, mod] + weights,
            [((4, LANES, HID), bf16), ((4, LANES, HID), f32), ((LANES, D), bf16)],
            fetch=(1, 2, 3, 4),
            store=(1, 2),
            parts={1: 4},
            flops=8 * D * HID * LANES,
        )

    with jax.named_scope("predict"):
        (part,) = call(
            predict_kernel, [place], [act, proj], [((8, C_OUT, LANES), f32)]
        )
        parts = swap(part, SHARERS)
        (shared,) = call(own_kernel, [], [parts], [((GROUPS, C_OUT, LANES), bf16)])
        base_rows, facts = call(
            base_kernel, [], [gathered, rows, head_all], [((C_OUT, LANES), f32), ((72, LANES), f32)],
            fetch=(1, 2),
            store=(0, 1),
        )
        shared = swap(shared, "expert")

    with jax.named_scope("backward"):
        (parcel,) = call(
            backward_kernel,
            [place],
            [shared, base_rows, facts, block, proj, slope, mod, head_all, rows]
            + weights,
            [((SHARDS, PACK, LANES), bf16)],
            fetch=(1, 2, 3, 4, 5, 9, 10, 11, 12, 13, 6, 7, 8),
            flops=8 * D * HID * LANES,
        )
        parcel = swap(parcel, FSDP)
        (home,) = call(mid_kernel, [], [parcel], [((GROUPS, 16, LANES), bf16)])
        (direct,) = call(direct_kernel, [], [parcel, head], [((FEAT, TOK), f32)])
        home = swap(home, "expert")

    with jax.named_scope("finish"):
        grad_tokens, loss = call(
            end_kernel,
            [place, levels],
            [home, pick, direct],
            [((FEAT, TOK), bf16), ((1, 1), f32)],
        )
    return (grad_tokens.T, loss.reshape(()))


def solution(mesh):
    mesh = Mesh(mesh.devices.reshape(4, 2, 4, 16), FSDP + ("expert",))
    in_specs = (
        P("expert", FSDP),
        P(),
        P("expert", None),
        P("expert", None),
        P("expert", None, FSDP),
        P("expert", FSDP, None),
        P(None, FSDP),
        P("expert", None),
        P(),
        P(),
        P(),
    )
    out_specs = (P("expert", FSDP), P())
    return jax.shard_map(local, mesh=mesh, in_specs=in_specs, out_specs=out_specs, check_vma=False)
```

```python
import functools
import math

import jax
import jax.numpy as jnp
from jax import lax
from jax.experimental import pallas as pl
from jax.experimental.pallas import tpu as pltpu
from jax.sharding import Mesh, PartitionSpec as P

D = 1792
TOPK = 2
C_OUT = 16
SAMPLES = 4
LANES = 128
FEAT = 56
SHARDS = 32
GROUPS = 16
CAP = 32
TOK = 256
HID = 224
PACK = 64
FSDP = ("y", "zh", "zl")
RING = ("zh", "zl")
SHARERS = ("y", "zh")


norm_eps = 1e-06
dpo_beta = 2.0
bf16 = jnp.bfloat16
f32 = jnp.float32
i32 = jnp.int32
highest = lax.Precision.HIGHEST
contract_last = (((1,), (1,)), ((), ()))
contract_first = (((0,), (0,)), ((), ()))


def dot(a, b, **kw):
    return jnp.dot(a, b, preferred_element_type=f32, **kw)


def dot_nt(a, b, **kw):
    return lax.dot_general(a, b, contract_last, preferred_element_type=f32, **kw)


def iota(shape, axis):
    return lax.broadcasted_iota(i32, shape, axis)


def high_low(values):
    high = values.astype(bf16).astype(f32)
    return high, values - high


def whole(weight):
    if isinstance(weight, tuple):
        return jnp.concatenate([part[...] for part in weight], axis=0)
    return weight[...]


def lane_blocks(tiles):
    block = iota(tiles[0].shape, 1) // CAP
    out = []
    for b in range(4):
        total = None
        for j in range(4):
            moved = tiles[j] if j == b else pltpu.roll(tiles[j], (CAP * (j - b)) % LANES, axis=1)
            total = moved if total is None else jnp.where(block == j, moved, total)
        out.append(total)
    return out


def routing_kernel(place_ref, tokens_ref, routes_ref, weights_ref, targets_ref, sent_ref, pick_ref):
    shard = place_ref[0]
    expert = iota((GROUPS, TOK), 0)
    hits = [(routes_ref[k : k + 1, :] == expert).astype(f32) for k in range(TOPK)]
    below = (iota((TOK, TOK), 0) < iota((TOK, TOK), 1)).astype(bf16)
    named = hits[0] + hits[1]
    earlier = dot(named.astype(bf16), below)
    slots = [jnp.sum(earlier * hit, axis=0, keepdims=True) for hit in hits]
    kept = [(slot < CAP).astype(f32) for slot in slots]
    lost = (1.0 - kept[0]) * (1.0 - kept[1])
    rank = dot(jnp.broadcast_to(lost, (8, TOK)).astype(bf16), below)[0:1]
    full = jnp.minimum(jnp.sum(named, axis=1, keepdims=True), float(CAP))
    empty = jnp.broadcast_to(CAP - full, (GROUPS, LANES))
    order = (iota((GROUPS, GROUPS), 1) < iota((GROUPS, GROUPS), 0)).astype(bf16)
    start = dot(order, empty.astype(bf16))[:, 0:1]
    inside = (rank >= start) & (rank < start + CAP - full)
    spare = jnp.where(inside, expert.astype(f32) * CAP + full + rank - start, 0.0)
    spare = jnp.sum(spare, axis=0, keepdims=True)
    lane = iota((GROUPS * CAP, TOK), 0)
    places = []
    for k in range(TOPK):
        dest = routes_ref[k : k + 1, :].astype(f32) * CAP + slots[k]
        dest = jnp.where(kept[k] > 0.5, dest, -1.0)
        if k == 0:
            dest = jnp.where(lost > 0.5, spare, dest)
        places.append((lane == dest.astype(i32)).astype(f32))
    pick_ref[...] = (places[0] + places[1]).astype(bf16)
    pick_ref.start()

    row = iota((PACK, LANES), 0)
    pick_fact = ((row == FEAT) & (iota((PACK, LANES), 1) == shard)).astype(bf16)
    body = jnp.concatenate(
        [tokens_ref[...].astype(f32), jnp.zeros((PACK - FEAT, TOK), f32)], axis=0
    )
    line = iota((8, TOK), 0)
    packed = None
    for k in range(TOPK):
        other = 1 - k
        own = high_low(weights_ref[k : k + 1, :] * kept[k])
        partner = high_low(weights_ref[other : other + 1, :] * kept[other])
        first = jnp.ones((1, TOK), f32) if k == 0 else 1.0 - kept[0]
        facts = [
            own[0], own[1], partner[0], partner[1],
            routes_ref[other : other + 1, :].astype(f32) * kept[other],
            slots[other] * kept[other],
            first,
        ]
        table = jnp.zeros((8, TOK), f32)
        for place, fact in enumerate(facts):
            table = jnp.where(line == place, fact, table)
        table = jnp.concatenate(
            [targets_ref[...], table, jnp.zeros((LANES - C_OUT - 8, TOK), f32)], axis=0
        )
        features = body + dot(pick_fact, table.astype(bf16))
        part = dot_nt(features.astype(bf16), places[k].astype(bf16))
        packed = part if packed is None else packed + part
    for tile in range(4):
        pieces = [
            packed[16 * j : 16 * j + 16, tile * LANES : (tile + 1) * LANES] for j in range(4)
        ]
        for b, piece in enumerate(lane_blocks(pieces)):
            sent_ref[4 * tile + b] = piece.astype(bf16)


def parcel_kernel(arrived_ref, head_ref, parcel_ref):
    row = iota((8, LANES), 0)
    head = head_ref[...].astype(f32)
    for q in range(4):
        tiles = lane_blocks([arrived_ref[4 * q + b].astype(f32) for b in range(4)])
        tail = jnp.where(row == 0, tiles[3][8:], head)
        body = jnp.concatenate([tiles[0], tiles[1], tiles[2], tiles[3][:8], tail], axis=0)
        body = body.astype(bf16)
        for high in range(8):
            parcel_ref[4 * high + q] = body


def head_kernel(gathered_ref, gate_ref, w_out_ref, proj_ref, head_ref):
    pieces = []
    for f in range(SHARDS):
        rows = gathered_ref[f, FEAT:PACK].astype(f32)
        for i in range(FEAT // 8):
            pieces.append(jnp.broadcast_to(rows[i + 1 : i + 2], (8, LANES)))
    spread = jnp.concatenate(pieces, axis=0)
    lane = iota((D, LANES), 1)
    spread = jnp.where(lane // C_OUT == iota((D, LANES), 0) % 8, spread, 0.0).astype(bf16)
    fold = iota((LANES, LANES), 0) % C_OUT == iota((LANES, LANES), 1) % C_OUT
    head = dot(spread, fold.astype(bf16))
    head_ref[...] = head.astype(bf16)
    head_ref.start()
    high, low = high_low(head * gate_ref[...])
    pair = jnp.where(lane < PACK, high, low).astype(bf16)
    proj = dot(w_out_ref[...], pair)
    proj = proj + pltpu.roll(proj, PACK, axis=1)
    proj = proj.T
    for z in range(8):
        q = z % SAMPLES
        proj_ref[z] = proj[C_OUT * q : C_OUT * (q + 1)].astype(bf16)


def first_kernel(
    place_ref, gathered_ref, mod_ref, w0_ref, w1_ref, w2_ref, w3_ref, w4_ref, act_ref, slope_ref, rows_ref
):
    rows = jnp.concatenate([gathered_ref[f, :FEAT].astype(f32) for f in range(SHARDS)], axis=0).T
    rows_ref[...] = rows.astype(bf16)
    rows_ref.start()
    rms = lax.rsqrt(jnp.sum(rows * rows, axis=1, keepdims=True) / D + norm_eps)
    mine = pl.ds(place_ref[1], 1)
    normed = (rows * rms) * (1.0 + mod_ref[1, mine, :]) + mod_ref[0, mine, :]
    normed = normed.astype(bf16)
    weights = [w0_ref, w1_ref, w2_ref, (w3_ref, w4_ref)]
    for b, weight in enumerate(weights):
        pre = dot_nt(normed, whole(weight))
        cubic = math.sqrt(2.0 / math.pi)
        square = pre * pre
        tanh = jnp.tanh(cubic * (pre + 0.044715 * square * pre))
        half = 0.5 * (1.0 + tanh)
        act_ref[b] = (pre * half).astype(bf16)
        slope_ref[b] = half + 0.5 * pre * (1.0 - tanh * tanh) * (
            cubic * (1.0 + 3.0 * 0.044715 * square)
        )
        slope_ref.start(b)


def held_projections(proj_ref, z):
    lane = iota((C_OUT, HID), 1)
    after, before = proj_ref[(z + 2) % 8].astype(f32), proj_ref[(z + 6) % 8].astype(f32)
    ends = jnp.where(lane < HID // 2, after, before).astype(bf16)
    return [proj_ref[z], proj_ref[(z + 7) % 8], proj_ref[(z + 1) % 8], ends]


def predict_kernel(place_ref, act_ref, proj_ref, part_ref):
    total = None
    for b, proj in enumerate(held_projections(proj_ref, place_ref[4])):
        part = dot_nt(proj, act_ref[b])
        total = part if total is None else total + part
    for other in range(8):
        part_ref[other] = total


def own_kernel(parts_ref, shared_ref):
    own = jnp.sum(parts_ref[...], axis=0).astype(bf16)
    for e in range(GROUPS):
        shared_ref[e] = own


def base_kernel(gathered_ref, rows_ref, head_ref, base_ref, facts_ref):
    base = dot(rows_ref[...], head_ref[...]).T
    base_ref[...] = base[:C_OUT]
    tails = [gathered_ref[f, FEAT:PACK].astype(f32)[:1] for f in range(SHARDS)]
    facts_ref[...] = jnp.concatenate(tails, axis=0)


def backward_kernel(
    place_ref, shared_ref, base_ref, facts_ref, proj_ref, slope_ref,
    mod_ref, head_ref, rows_ref, w0_ref, w1_ref, w2_ref, w3_ref, w4_ref, parcel_ref,
):
    quarter, leader = place_ref[1], place_ref[2]
    facts = facts_ref[...]
    target = facts[:C_OUT]
    own_w = facts[16:17] + facts[17:18]
    other_w = facts[18:19] + facts[19:20]
    first = facts[22:23]
    lane = iota((1, LANES), 1)
    source = facts[20:21].astype(i32) * LANES + facts[21:22].astype(i32) + lane // CAP * CAP
    chosen = (iota((GROUPS * LANES, LANES), 0) == source).astype(f32).astype(bf16)
    everyone = jnp.concatenate([shared_ref[e] for e in range(GROUPS)], axis=1)
    partner = dot(everyone, chosen)
    residue = base_ref[...] + own_w * shared_ref[place_ref[5]].astype(f32) + other_w * partner - target
    kept_err = jnp.sum(first * residue * residue, keepdims=True)

    err = jnp.where((lane == quarter) & (leader == 1), kept_err, 0.0)
    row = iota((8, LANES), 0)
    tail = jnp.zeros((8, LANES), f32)
    for place, values in enumerate(high_low(err)):
        tail = jnp.where(row == place, values, tail)

    upstream = jnp.concatenate(high_low((own_w * residue).T), axis=1).astype(bf16)
    weights = [w0_ref, w1_ref, w2_ref, (w3_ref, w4_ref)]
    total = None
    for b, proj in enumerate(held_projections(proj_ref, place_ref[4])):
        grad = slope_ref[b] * dot(upstream, jnp.concatenate([proj, proj], axis=0))
        part = dot(grad.astype(bf16), whole(weights[b]))
        total = part if total is None else total + part
    rows = rows_ref[...].astype(f32)
    rms = lax.rsqrt(jnp.sum(rows * rows, axis=1, keepdims=True) / D + norm_eps)
    total = total * (rms * (1.0 + mod_ref[1, pl.ds(quarter, 1), :]))
    inner = jnp.sum(total * rows, axis=1, keepdims=True) * (rms * rms / D)
    high, low = high_low(first * residue * 0.125)
    direct = jnp.concatenate([high, low, jnp.zeros((LANES - 2 * C_OUT, LANES), f32)], axis=0)
    total = total - rows * inner + dot_nt(direct.T.astype(bf16), head_ref[...])
    total = total.T
    for f in range(SHARDS):
        parcel_ref[f] = jnp.concatenate(
            [total[FEAT * f : FEAT * (f + 1)], tail], axis=0
        ).astype(bf16)


def mid_kernel(parcel_ref, home_ref):
    lane = iota((1, LANES), 1)
    row = iota((8, LANES), 0)
    sums, tails = [], []
    for q in range(4):
        total = None
        for high in range(8):
            f = 4 * high + q
            part = parcel_ref[f].astype(f32)
            total = part if total is None else total + part
        sums.append(total[:FEAT])
        tails.append(total[FEAT:])
    tail = tails[0] + tails[1] + tails[2] + tails[3]
    err = jnp.where(lane < SAMPLES, tail[0:1] + tail[1:2], 0.0)
    err = err + pltpu.roll(err, CAP, axis=1)
    err = err + pltpu.roll(err, 2 * CAP, axis=1)
    high, low = high_low(err)
    tail = jnp.where(row == 0, high, 0.0) + jnp.where(row == 1, low, 0.0)
    for q in range(4):
        full = jnp.concatenate([sums[q], tail], axis=0)
        tiles = lane_blocks([full[16 * j : 16 * j + 16] for j in range(4)])
        for b in range(4):
            home_ref[4 * q + b] = tiles[b].astype(bf16)


def end_kernel(
    place_ref, levels_ref, home_ref, pick_ref,
    grad_ref, loss_ref,
):
    sample = place_ref[3].astype(f32)
    pairs = [levels_ref[SAMPLES + 2 + i] for i in range(SAMPLES)]
    columns = []
    for tile in range(4):
        tiles = lane_blocks([home_ref[4 * tile + b].astype(f32) for b in range(4)])
        columns.append(jnp.concatenate(tiles, axis=0))
    home = jnp.concatenate(columns, axis=1)
    back = dot(home.astype(bf16), pick_ref[...])
    err = functools.reduce(jnp.add, [column[FEAT : FEAT + 1] for column in columns])
    err = err + functools.reduce(jnp.add, [column[FEAT + 1 : FEAT + 2] for column in columns])
    err = jnp.broadcast_to(err, (8, LANES)) / (TOK * GROUPS // SAMPLES * C_OUT)
    lane = iota((8, LANES), 1) % CAP
    excess = []
    for s in range(SAMPLES):
        total = jnp.sum(jnp.where(lane == s, err, 0.0), axis=1, keepdims=True)
        excess.append(jnp.broadcast_to(total, (8, LANES)) - levels_ref[s])
    loss, coef = 0.0, 0.0
    for k in range(2):
        winner, loser = pairs[2 * k], pairs[2 * k + 1]
        margin = 0.0
        for s in range(SAMPLES):
            margin = margin + jnp.where(winner == s, excess[s], 0.0)
        for s in range(SAMPLES):
            margin = margin - jnp.where(loser == s, excess[s], 0.0)
        down = levels_ref[SAMPLES + k] * margin
        loss = loss + jnp.maximum(down, 0.0) + jnp.log1p(jnp.exp(-jnp.abs(down)))
        rate = levels_ref[SAMPLES + k] / (1.0 + jnp.exp(-down)) * 0.5
        coef = coef + jnp.where(winner == sample, rate, 0.0)
        coef = coef - jnp.where(loser == sample, rate, 0.0)
    loss_ref[...] = loss[0:1, 0:1] * 0.5
    coef = coef[0:1, 0:1] * (TOK * GROUPS * C_OUT * 2.0 / (TOK * GROUPS // SAMPLES * C_OUT))
    grad_ref[...] = (coef * back[:FEAT]).astype(bf16)


class Fetched:
    def __init__(self, source, held, semaphore):
        self.held = held
        self.copy = pltpu.make_async_copy(source, held, semaphore)
        self.copy.start()

    def wait(self):
        if self.copy is not None:
            self.copy.wait()
            self.copy = None

    def __getitem__(self, index):
        self.wait()
        return self.held[index]


class Stored:
    def __init__(self, target, held, semaphore, parts):
        self.held = held
        if parts == 1:
            self.copies = [pltpu.make_async_copy(held, target, semaphore.at[0])]
        else:
            self.copies = [
                pltpu.make_async_copy(held.at[i], target.at[i], semaphore.at[i])
                for i in range(parts)
            ]
        self.started = [False] * parts

    def __setitem__(self, index, values):
        self.held[index] = values

    def start(self, part=0):
        if not self.started[part]:
            self.copies[part].start()
            self.started[part] = True

    def finish(self):
        for part in range(len(self.copies)):
            self.start(part)

    def wait(self):
        for copy in self.copies:
            copy.wait()


def call(kernel, scalars, arrays, outs, fetch=(), store=(), parts={}, flops=0):
    vmem = pl.BlockSpec(memory_space=pltpu.VMEM)
    smem = pl.BlockSpec(memory_space=pltpu.SMEM)
    hbm = pl.BlockSpec(memory_space=pltpu.HBM)
    size = sum(a.size * a.dtype.itemsize for a in arrays)
    out_shape = [
        pltpu.HBM(shape, dtype) if i in store else jax.ShapeDtypeStruct(shape, dtype)
        for i, (shape, dtype) in enumerate(outs)
    ]
    arrays = [
        pltpu.with_memory_space_constraint(a, pltpu.HBM) if i in fetch else a
        for i, a in enumerate(arrays)
    ]
    moved = [arrays[i] for i in fetch] + [out_shape[i] for i in store]
    scratch = [pltpu.VMEM(a.shape, a.dtype) for a in moved]
    counts = [1] * len(fetch) + [parts.get(i, 1) for i in store]
    starts = [sum(counts[:n]) for n in range(len(counts))]
    if moved:
        scratch.append(pltpu.SemaphoreType.DMA((sum(counts),)))

    def body(*refs):
        refs = list(refs)
        at_in = len(scalars)
        at_out = at_in + len(arrays)
        at_held = at_out + len(outs)
        fetched, stored = [], []
        for n, i in enumerate(fetch):
            fetched.append(Fetched(refs[at_in + i], refs[at_held + n], refs[-1].at[n]))
            refs[at_in + i] = fetched[-1]
        for n, i in enumerate(store, len(fetch)):
            semaphores = refs[-1].at[pl.ds(starts[n], counts[n])]
            stored.append(Stored(refs[at_out + i], refs[at_held + n], semaphores, counts[n]))
            refs[at_out + i] = stored[-1]
        kernel(*refs[:at_held])
        for item in stored:
            item.finish()
        for item in fetched + stored:
            item.wait()

    return pl.pallas_call(
        body,
        out_shape=out_shape,
        in_specs=[smem] * len(scalars)
        + [hbm if i in fetch else vmem for i in range(len(arrays))],
        out_specs=[hbm if i in store else vmem for i in range(len(outs))],
        scratch_shapes=scratch,
        compiler_params=pltpu.CompilerParams(vmem_limit_bytes=24 * 1024 * 1024),
        cost_estimate=pl.CostEstimate(flops=flops, bytes_accessed=size, transcendentals=0),
    )(*scalars, *arrays)


def swap(chunks, axis):
    return lax.all_to_all(chunks, axis, split_axis=0, concat_axis=0, tiled=True)


def local(
    tokens,
    modulation,
    routes,
    route_weights,
    w_first,
    w_second,
    head,
    targets,
    ref_err,
    pair_ids,
    timesteps,
):
    shard = lax.axis_index(FSDP)
    ring = lax.axis_index(RING)
    quarter = lax.axis_index("zl")
    leader = (lax.axis_index(SHARERS) == 0).astype(i32)
    my_sample = lax.axis_index("expert") * SAMPLES // GROUPS
    place = jnp.stack([shard, quarter, leader, my_sample, ring, lax.axis_index("expert")]).astype(i32)
    fraction = timesteps.astype(f32) / 1000.0
    keep_level = jnp.cos((fraction + 0.008) / 1.008 * (math.pi / 2.0)) ** 2
    levels = jnp.concatenate([ref_err, dpo_beta * keep_level, pair_ids.astype(f32)])
    w_in = w_first[0].T
    mod = modulation.transpose(1, 0, 2)

    with jax.named_scope("weights"):
        up = [(z, (z + 1) % 8) for z in range(8)]
        down = [(z, (z + 7) % 8) for z in range(8)]
        w_before = lax.ppermute(w_in, RING, up)
        w_after = lax.ppermute(w_in, RING, down)

    with jax.named_scope("routing"):
        sent, pick = call(
            routing_kernel,
            [place],
            [tokens.T, routes.T, route_weights.T, targets.T],
            [((GROUPS, 16, LANES), bf16), ((GROUPS * CAP, TOK), bf16)],
            store=(1,),
        )
    with jax.named_scope("dispatch"):
        arrived = swap(sent, "expert")
        arrived, w_before, w_after = lax.optimization_barrier((arrived, w_before, w_after))
        half = HID // 2
        weights = [
            w_in,
            w_before,
            w_after,
            lax.ppermute(w_after[:half], RING, down),
            lax.ppermute(w_before[half:], RING, up),
        ]
        head_flat = jnp.pad(head.T.reshape(FEAT // 8, LANES), ((1, 0), (0, 0)))
        (parcel,) = call(parcel_kernel, [], [arrived, head_flat], [((SHARDS, PACK, LANES), bf16)])
        gathered = swap(parcel, FSDP)

    with jax.named_scope("projection"):
        gate = jnp.tile(jnp.repeat(mod[2].T, C_OUT, axis=1), (1, 2))
        proj, head_all = call(
            head_kernel,
            [],
            [gathered, gate, w_second[0]],
            [((8, C_OUT, HID), bf16), ((D, LANES), bf16)],
            store=(0, 1),
        )
        proj = swap(proj, RING)

    with jax.named_scope("first_layer"):
        act, slope, rows = call(
            first_kernel,
            [place],
            [gathered, mod] + weights,
            [((4, LANES, HID), bf16), ((4, LANES, HID), f32), ((LANES, D), bf16)],
            fetch=(1, 2, 3, 4),
            store=(1, 2),
            parts={1: 4},
            flops=8 * D * HID * LANES,
        )

    with jax.named_scope("predict"):
        (part,) = call(
            predict_kernel, [place], [act, proj], [((8, C_OUT, LANES), f32)]
        )
        parts = swap(part, SHARERS)
        (shared,) = call(own_kernel, [], [parts], [((GROUPS, C_OUT, LANES), bf16)])
        base_rows, facts = call(
            base_kernel, [], [gathered, rows, head_all], [((C_OUT, LANES), f32), ((SHARDS, LANES), f32)],
            fetch=(1, 2),
            store=(0, 1),
        )
        shared = swap(shared, "expert")

    with jax.named_scope("backward"):
        (parcel,) = call(
            backward_kernel,
            [place],
            [shared, base_rows, facts, proj, slope, mod, head_all, rows]
            + weights,
            [((SHARDS, PACK, LANES), bf16)],
            fetch=(1, 2, 3, 4, 8, 9, 10, 11, 12, 5, 6, 7),
            flops=8 * D * HID * LANES,
        )
        parcel = swap(parcel, FSDP)
        (home,) = call(mid_kernel, [], [parcel], [((GROUPS, 16, LANES), bf16)])
        home = swap(home, "expert")

    with jax.named_scope("finish"):
        grad_tokens, loss = call(
            end_kernel,
            [place, levels],
            [home, pick],
            [((FEAT, TOK), bf16), ((1, 1), f32)],
        )
    return (grad_tokens.T, loss.reshape(()))


def solution(mesh):
    mesh = Mesh(mesh.devices.reshape(4, 2, 4, 16), FSDP + ("expert",))
    in_specs = (
        P("expert", FSDP),
        P(),
        P("expert", None),
        P("expert", None),
        P("expert", None, FSDP),
        P("expert", FSDP, None),
        P(None, FSDP),
        P("expert", None),
        P(),
        P(),
        P(),
    )
    out_specs = (P("expert", FSDP), P())
    return jax.shard_map(local, mesh=mesh, in_specs=in_specs, out_specs=out_specs, check_vma=False)
```

```python
import functools
import math

import jax
import jax.numpy as jnp
from jax import lax
from jax.experimental import pallas as pl
from jax.experimental.pallas import tpu as pltpu
from jax.sharding import Mesh, PartitionSpec as P

D = 1792
TOPK = 2
C_OUT = 16
SAMPLES = 4
LANES = 128
FEAT = 56
SHARDS = 32
GROUPS = 16
CAP = 32
TOK = 256
HID = 224
PACK = 64
FSDP = ("y", "zh", "zl")
RING = ("zh", "zl")
SHARERS = ("y", "zh")


norm_eps = 1e-06
dpo_beta = 2.0
bf16 = jnp.bfloat16
f32 = jnp.float32
i32 = jnp.int32
highest = lax.Precision.HIGHEST
contract_last = (((1,), (1,)), ((), ()))
contract_first = (((0,), (0,)), ((), ()))


def dot(a, b, **kw):
    return jnp.dot(a, b, preferred_element_type=f32, **kw)


def dot_nt(a, b, **kw):
    return lax.dot_general(a, b, contract_last, preferred_element_type=f32, **kw)


def iota(shape, axis):
    return lax.broadcasted_iota(i32, shape, axis)


def high_low(values):
    high = values.astype(bf16).astype(f32)
    return high, values - high


def whole(weight):
    if isinstance(weight, tuple):
        return jnp.concatenate([part[...] for part in weight], axis=0)
    return weight[...]


def lane_blocks(tiles):
    block = iota(tiles[0].shape, 1) // CAP
    out = []
    for b in range(4):
        total = None
        for j in range(4):
            moved = tiles[j] if j == b else pltpu.roll(tiles[j], (CAP * (j - b)) % LANES, axis=1)
            total = moved if total is None else jnp.where(block == j, moved, total)
        out.append(total)
    return out


def routing_kernel(place_ref, tokens_ref, routes_ref, weights_ref, targets_ref, sent_ref, pick_ref):
    shard = place_ref[0]
    expert = iota((GROUPS, TOK), 0)
    hits = [(routes_ref[k : k + 1, :] == expert).astype(f32) for k in range(TOPK)]
    below = (iota((TOK, TOK), 0) < iota((TOK, TOK), 1)).astype(bf16)
    named = hits[0] + hits[1]
    earlier = dot(named.astype(bf16), below)
    slots = [jnp.sum(earlier * hit, axis=0, keepdims=True) for hit in hits]
    kept = [(slot < CAP).astype(f32) for slot in slots]
    lost = (1.0 - kept[0]) * (1.0 - kept[1])
    rank = dot(jnp.broadcast_to(lost, (8, TOK)).astype(bf16), below)[0:1]
    full = jnp.minimum(jnp.sum(named, axis=1, keepdims=True), float(CAP))
    empty = jnp.broadcast_to(CAP - full, (GROUPS, LANES))
    order = (iota((GROUPS, GROUPS), 1) < iota((GROUPS, GROUPS), 0)).astype(bf16)
    start = dot(order, empty.astype(bf16))[:, 0:1]
    inside = (rank >= start) & (rank < start + CAP - full)
    spare = jnp.where(inside, expert.astype(f32) * CAP + full + rank - start, 0.0)
    spare = jnp.sum(spare, axis=0, keepdims=True)
    lane = iota((GROUPS * CAP, TOK), 0)
    places = []
    for k in range(TOPK):
        dest = routes_ref[k : k + 1, :].astype(f32) * CAP + slots[k]
        dest = jnp.where(kept[k] > 0.5, dest, -1.0)
        if k == 0:
            dest = jnp.where(lost > 0.5, spare, dest)
        places.append((lane == dest.astype(i32)).astype(f32))
    pick_ref[...] = (places[0] + places[1]).astype(bf16)
    pick_ref.start()

    row = iota((PACK, LANES), 0)
    pick_fact = ((row == FEAT) & (iota((PACK, LANES), 1) == shard)).astype(bf16)
    body = jnp.concatenate(
        [tokens_ref[...].astype(f32), jnp.zeros((PACK - FEAT, TOK), f32)], axis=0
    )
    line = iota((8, TOK), 0)
    packed = None
    for k in range(TOPK):
        other = 1 - k
        own = high_low(weights_ref[k : k + 1, :] * kept[k])
        partner = high_low(weights_ref[other : other + 1, :] * kept[other])
        first = jnp.ones((1, TOK), f32) if k == 0 else 1.0 - kept[0]
        facts = [
            own[0], own[1], partner[0], partner[1],
            routes_ref[other : other + 1, :].astype(f32) * kept[other],
            slots[other] * kept[other],
            first,
        ]
        table = jnp.zeros((8, TOK), f32)
        for place, fact in enumerate(facts):
            table = jnp.where(line == place, fact, table)
        table = jnp.concatenate(
            [targets_ref[...], table, jnp.zeros((LANES - C_OUT - 8, TOK), f32)], axis=0
        )
        features = body + dot(pick_fact, table.astype(bf16))
        part = dot_nt(features.astype(bf16), places[k].astype(bf16))
        packed = part if packed is None else packed + part
    for tile in range(4):
        pieces = [
            packed[16 * j : 16 * j + 16, tile * LANES : (tile + 1) * LANES] for j in range(4)
        ]
        for b, piece in enumerate(lane_blocks(pieces)):
            sent_ref[4 * tile + b] = piece.astype(bf16)


def parcel_kernel(arrived_ref, head_ref, parcel_ref):
    row = iota((8, LANES), 0)
    head = head_ref[...].astype(f32)
    for q in range(4):
        tiles = lane_blocks([arrived_ref[4 * q + b].astype(f32) for b in range(4)])
        tail = jnp.where(row == 0, tiles[3][8:], head)
        body = jnp.concatenate([tiles[0], tiles[1], tiles[2], tiles[3][:8], tail], axis=0)
        body = body.astype(bf16)
        for high in range(8):
            parcel_ref[4 * high + q] = body


def head_kernel(gathered_ref, gate_ref, w_out_ref, proj_ref, head_ref):
    pieces = []
    for f in range(SHARDS):
        rows = gathered_ref[f, FEAT:PACK].astype(f32)
        for i in range(FEAT // 8):
            pieces.append(jnp.broadcast_to(rows[i + 1 : i + 2], (8, LANES)))
    spread = jnp.concatenate(pieces, axis=0)
    lane = iota((D, LANES), 1)
    spread = jnp.where(lane // C_OUT == iota((D, LANES), 0) % 8, spread, 0.0).astype(bf16)
    fold = iota((LANES, LANES), 0) % C_OUT == iota((LANES, LANES), 1) % C_OUT
    head = dot(spread, fold.astype(bf16))
    head_ref[...] = head.astype(bf16)
    head_ref.start()
    high, low = high_low(head * gate_ref[...])
    pair = jnp.where(lane < PACK, high, low).astype(bf16)
    proj = dot(w_out_ref[...], pair)
    proj = proj + pltpu.roll(proj, PACK, axis=1)
    proj = proj.T
    for z in range(8):
        q = z % SAMPLES
        proj_ref[z] = proj[C_OUT * q : C_OUT * (q + 1)].astype(bf16)


def first_kernel(
    place_ref, gathered_ref, mod_ref, w0_ref, w1_ref, w2_ref, w3_ref, w4_ref, head_ref,
    act_ref, slope_ref, rows_ref, base_ref, facts_ref,
):
    rows = jnp.concatenate([gathered_ref[f, :FEAT].astype(f32) for f in range(SHARDS)], axis=0).T
    rows_ref[...] = rows.astype(bf16)
    rows_ref.start()
    rms = lax.rsqrt(jnp.sum(rows * rows, axis=1, keepdims=True) / D + norm_eps)
    mine = pl.ds(place_ref[1], 1)
    normed = (rows * rms) * (1.0 + mod_ref[1, mine, :]) + mod_ref[0, mine, :]
    normed = normed.astype(bf16)
    weights = [w0_ref, w1_ref, w2_ref, (w3_ref, w4_ref)]
    for b, weight in enumerate(weights):
        pre = dot_nt(normed, whole(weight))
        cubic = math.sqrt(2.0 / math.pi)
        square = pre * pre
        tanh = jnp.tanh(cubic * (pre + 0.044715 * square * pre))
        half = 0.5 * (1.0 + tanh)
        act_ref[b] = (pre * half).astype(bf16)
        slope_ref[b] = half + 0.5 * pre * (1.0 - tanh * tanh) * (
            cubic * (1.0 + 3.0 * 0.044715 * square)
        )
        slope_ref.start(b)
    base_ref[...] = dot(rows.astype(bf16), head_ref[...]).T[:C_OUT]
    tails = [gathered_ref[f, FEAT:PACK].astype(f32)[:1] for f in range(SHARDS)]
    facts_ref[...] = jnp.concatenate(tails, axis=0)


def held_projections(proj_ref, z):
    lane = iota((C_OUT, HID), 1)
    after, before = proj_ref[(z + 2) % 8].astype(f32), proj_ref[(z + 6) % 8].astype(f32)
    ends = jnp.where(lane < HID // 2, after, before).astype(bf16)
    return [proj_ref[z], proj_ref[(z + 7) % 8], proj_ref[(z + 1) % 8], ends]


def predict_kernel(place_ref, act_ref, proj_ref, part_ref):
    total = None
    for b, proj in enumerate(held_projections(proj_ref, place_ref[4])):
        part = dot_nt(proj, act_ref[b])
        total = part if total is None else total + part
    for other in range(8):
        part_ref[other] = total


def own_kernel(parts_ref, shared_ref):
    own = jnp.sum(parts_ref[...], axis=0).astype(bf16)
    for e in range(GROUPS):
        shared_ref[e] = own


def backward_kernel(
    place_ref, shared_ref, base_ref, facts_ref, proj_ref, slope_ref,
    mod_ref, head_ref, rows_ref, w0_ref, w1_ref, w2_ref, w3_ref, w4_ref, parcel_ref,
):
    quarter, leader = place_ref[1], place_ref[2]
    facts = facts_ref[...]
    target = facts[:C_OUT]
    own_w = facts[16:17] + facts[17:18]
    other_w = facts[18:19] + facts[19:20]
    first = facts[22:23]
    lane = iota((1, LANES), 1)
    source = facts[20:21].astype(i32) * LANES + facts[21:22].astype(i32) + lane // CAP * CAP
    chosen = (iota((GROUPS * LANES, LANES), 0) == source).astype(f32).astype(bf16)
    everyone = jnp.concatenate([shared_ref[e] for e in range(GROUPS)], axis=1)
    partner = dot(everyone, chosen)
    residue = base_ref[...] + own_w * shared_ref[place_ref[5]].astype(f32) + other_w * partner - target
    kept_err = jnp.sum(first * residue * residue, keepdims=True)

    err = jnp.where((lane == quarter) & (leader == 1), kept_err, 0.0)
    row = iota((8, LANES), 0)
    tail = jnp.zeros((8, LANES), f32)
    for place, values in enumerate(high_low(err)):
        tail = jnp.where(row == place, values, tail)

    upstream = jnp.concatenate(high_low((own_w * residue).T), axis=1).astype(bf16)
    weights = [w0_ref, w1_ref, w2_ref, (w3_ref, w4_ref)]
    total = None
    for b, proj in enumerate(held_projections(proj_ref, place_ref[4])):
        grad = slope_ref[b] * dot(upstream, jnp.concatenate([proj, proj], axis=0))
        part = dot(grad.astype(bf16), whole(weights[b]))
        total = part if total is None else total + part
    rows = rows_ref[...].astype(f32)
    rms = lax.rsqrt(jnp.sum(rows * rows, axis=1, keepdims=True) / D + norm_eps)
    total = total * (rms * (1.0 + mod_ref[1, pl.ds(quarter, 1), :]))
    inner = jnp.sum(total * rows, axis=1, keepdims=True) * (rms * rms / D)
    high, low = high_low(first * residue * 0.125)
    direct = jnp.concatenate([high, low, jnp.zeros((LANES - 2 * C_OUT, LANES), f32)], axis=0)
    total = total - rows * inner + dot_nt(direct.T.astype(bf16), head_ref[...])
    total = total.T
    for f in range(SHARDS):
        parcel_ref[f] = jnp.concatenate(
            [total[FEAT * f : FEAT * (f + 1)], tail], axis=0
        ).astype(bf16)


def mid_kernel(parcel_ref, home_ref):
    lane = iota((1, LANES), 1)
    row = iota((8, LANES), 0)
    sums, tails = [], []
    for q in range(4):
        total = None
        for high in range(8):
            f = 4 * high + q
            part = parcel_ref[f].astype(f32)
            total = part if total is None else total + part
        sums.append(total[:FEAT])
        tails.append(total[FEAT:])
    tail = tails[0] + tails[1] + tails[2] + tails[3]
    err = jnp.where(lane < SAMPLES, tail[0:1] + tail[1:2], 0.0)
    err = err + pltpu.roll(err, CAP, axis=1)
    err = err + pltpu.roll(err, 2 * CAP, axis=1)
    high, low = high_low(err)
    tail = jnp.where(row == 0, high, 0.0) + jnp.where(row == 1, low, 0.0)
    for q in range(4):
        full = jnp.concatenate([sums[q], tail], axis=0)
        tiles = lane_blocks([full[16 * j : 16 * j + 16] for j in range(4)])
        for b in range(4):
            home_ref[4 * q + b] = tiles[b].astype(bf16)


def end_kernel(
    place_ref, levels_ref, home_ref, pick_ref,
    grad_ref, loss_ref,
):
    sample = place_ref[3].astype(f32)
    pairs = [levels_ref[SAMPLES + 2 + i] for i in range(SAMPLES)]
    columns = []
    for tile in range(4):
        tiles = lane_blocks([home_ref[4 * tile + b].astype(f32) for b in range(4)])
        columns.append(jnp.concatenate(tiles, axis=0))
    home = jnp.concatenate(columns, axis=1)
    back = dot(home.astype(bf16), pick_ref[...])
    err = functools.reduce(jnp.add, [column[FEAT : FEAT + 1] for column in columns])
    err = err + functools.reduce(jnp.add, [column[FEAT + 1 : FEAT + 2] for column in columns])
    err = jnp.broadcast_to(err, (8, LANES)) / (TOK * GROUPS // SAMPLES * C_OUT)
    lane = iota((8, LANES), 1) % CAP
    excess = []
    for s in range(SAMPLES):
        total = jnp.sum(jnp.where(lane == s, err, 0.0), axis=1, keepdims=True)
        excess.append(jnp.broadcast_to(total, (8, LANES)) - levels_ref[s])
    loss, coef = 0.0, 0.0
    for k in range(2):
        winner, loser = pairs[2 * k], pairs[2 * k + 1]
        margin = 0.0
        for s in range(SAMPLES):
            margin = margin + jnp.where(winner == s, excess[s], 0.0)
        for s in range(SAMPLES):
            margin = margin - jnp.where(loser == s, excess[s], 0.0)
        down = levels_ref[SAMPLES + k] * margin
        loss = loss + jnp.maximum(down, 0.0) + jnp.log1p(jnp.exp(-jnp.abs(down)))
        rate = levels_ref[SAMPLES + k] / (1.0 + jnp.exp(-down)) * 0.5
        coef = coef + jnp.where(winner == sample, rate, 0.0)
        coef = coef - jnp.where(loser == sample, rate, 0.0)
    loss_ref[...] = loss[0:1, 0:1] * 0.5
    coef = coef[0:1, 0:1] * (TOK * GROUPS * C_OUT * 2.0 / (TOK * GROUPS // SAMPLES * C_OUT))
    grad_ref[...] = (coef * back[:FEAT]).astype(bf16)


class Fetched:
    def __init__(self, source, held, semaphore):
        self.held = held
        self.copy = pltpu.make_async_copy(source, held, semaphore)
        self.copy.start()

    def wait(self):
        if self.copy is not None:
            self.copy.wait()
            self.copy = None

    def __getitem__(self, index):
        self.wait()
        return self.held[index]


class Stored:
    def __init__(self, target, held, semaphore, parts):
        self.held = held
        if parts == 1:
            self.copies = [pltpu.make_async_copy(held, target, semaphore.at[0])]
        else:
            self.copies = [
                pltpu.make_async_copy(held.at[i], target.at[i], semaphore.at[i])
                for i in range(parts)
            ]
        self.started = [False] * parts

    def __setitem__(self, index, values):
        self.held[index] = values

    def start(self, part=0):
        if not self.started[part]:
            self.copies[part].start()
            self.started[part] = True

    def finish(self):
        for part in range(len(self.copies)):
            self.start(part)

    def wait(self):
        for copy in self.copies:
            copy.wait()


def call(kernel, scalars, arrays, outs, fetch=(), store=(), parts={}, flops=0):
    vmem = pl.BlockSpec(memory_space=pltpu.VMEM)
    smem = pl.BlockSpec(memory_space=pltpu.SMEM)
    hbm = pl.BlockSpec(memory_space=pltpu.HBM)
    size = sum(a.size * a.dtype.itemsize for a in arrays)
    out_shape = [
        pltpu.HBM(shape, dtype) if i in store else jax.ShapeDtypeStruct(shape, dtype)
        for i, (shape, dtype) in enumerate(outs)
    ]
    arrays = [
        pltpu.with_memory_space_constraint(a, pltpu.HBM) if i in fetch else a
        for i, a in enumerate(arrays)
    ]
    moved = [arrays[i] for i in fetch] + [out_shape[i] for i in store]
    scratch = [pltpu.VMEM(a.shape, a.dtype) for a in moved]
    counts = [1] * len(fetch) + [parts.get(i, 1) for i in store]
    starts = [sum(counts[:n]) for n in range(len(counts))]
    if moved:
        scratch.append(pltpu.SemaphoreType.DMA((sum(counts),)))

    def body(*refs):
        refs = list(refs)
        at_in = len(scalars)
        at_out = at_in + len(arrays)
        at_held = at_out + len(outs)
        fetched, stored = [], []
        for n, i in enumerate(fetch):
            fetched.append(Fetched(refs[at_in + i], refs[at_held + n], refs[-1].at[n]))
            refs[at_in + i] = fetched[-1]
        for n, i in enumerate(store, len(fetch)):
            semaphores = refs[-1].at[pl.ds(starts[n], counts[n])]
            stored.append(Stored(refs[at_out + i], refs[at_held + n], semaphores, counts[n]))
            refs[at_out + i] = stored[-1]
        kernel(*refs[:at_held])
        for item in stored:
            item.finish()
        for item in fetched + stored:
            item.wait()

    return pl.pallas_call(
        body,
        out_shape=out_shape,
        in_specs=[smem] * len(scalars)
        + [hbm if i in fetch else vmem for i in range(len(arrays))],
        out_specs=[hbm if i in store else vmem for i in range(len(outs))],
        scratch_shapes=scratch,
        compiler_params=pltpu.CompilerParams(vmem_limit_bytes=24 * 1024 * 1024),
        cost_estimate=pl.CostEstimate(flops=flops, bytes_accessed=size, transcendentals=0),
    )(*scalars, *arrays)


def swap(chunks, axis):
    return lax.all_to_all(chunks, axis, split_axis=0, concat_axis=0, tiled=True)


def local(
    tokens,
    modulation,
    routes,
    route_weights,
    w_first,
    w_second,
    head,
    targets,
    ref_err,
    pair_ids,
    timesteps,
):
    shard = lax.axis_index(FSDP)
    ring = lax.axis_index(RING)
    quarter = lax.axis_index("zl")
    leader = (lax.axis_index(SHARERS) == 0).astype(i32)
    my_sample = lax.axis_index("expert") * SAMPLES // GROUPS
    place = jnp.stack([shard, quarter, leader, my_sample, ring, lax.axis_index("expert")]).astype(i32)
    fraction = timesteps.astype(f32) / 1000.0
    keep_level = jnp.cos((fraction + 0.008) / 1.008 * (math.pi / 2.0)) ** 2
    levels = jnp.concatenate([ref_err, dpo_beta * keep_level, pair_ids.astype(f32)])
    w_in = w_first[0].T
    mod = modulation.transpose(1, 0, 2)

    with jax.named_scope("weights"):
        up = [(z, (z + 1) % 8) for z in range(8)]
        down = [(z, (z + 7) % 8) for z in range(8)]
        w_before = lax.ppermute(w_in, RING, up)
        w_after = lax.ppermute(w_in, RING, down)

    with jax.named_scope("routing"):
        sent, pick = call(
            routing_kernel,
            [place],
            [tokens.T, routes.T, route_weights.T, targets.T],
            [((GROUPS, 16, LANES), bf16), ((GROUPS * CAP, TOK), bf16)],
            store=(1,),
        )
    with jax.named_scope("dispatch"):
        head_flat = jnp.pad(head.T.reshape(FEAT // 8, LANES), ((1, 0), (0, 0)))
        sent, head_flat = lax.optimization_barrier((sent, head_flat))
        arrived = swap(sent, "expert")
        arrived, w_before, w_after = lax.optimization_barrier((arrived, w_before, w_after))
        half = HID // 2
        weights = [
            w_in,
            w_before,
            w_after,
            lax.ppermute(w_after[:half], RING, down),
            lax.ppermute(w_before[half:], RING, up),
        ]
        (parcel,) = call(parcel_kernel, [], [arrived, head_flat], [((SHARDS, PACK, LANES), bf16)])
        gathered, levels = lax.optimization_barrier((swap(parcel, FSDP), levels))

    with jax.named_scope("projection"):
        gate = jnp.tile(jnp.repeat(mod[2].T, C_OUT, axis=1), (1, 2))
        proj, head_all = call(
            head_kernel,
            [],
            [gathered, gate, w_second[0]],
            [((8, C_OUT, HID), bf16), ((D, LANES), bf16)],
            store=(0, 1),
        )
        proj = swap(proj, RING)

    with jax.named_scope("first_layer"):
        act, slope, rows, base_rows, facts = call(
            first_kernel,
            [place],
            [gathered, mod] + weights + [head_all],
            [((4, LANES, HID), bf16), ((4, LANES, HID), f32), ((LANES, D), bf16), ((C_OUT, LANES), f32), ((SHARDS, LANES), f32)],
            fetch=(1, 2, 3, 4, 7),
            store=(1, 2, 3, 4),
            parts={1: 4},
            flops=8 * D * HID * LANES,
        )

    with jax.named_scope("predict"):
        (part,) = call(
            predict_kernel, [place], [act, proj], [((8, C_OUT, LANES), f32)]
        )
        parts = swap(part, SHARERS)
        (shared,) = call(own_kernel, [], [parts], [((GROUPS, C_OUT, LANES), bf16)])
        shared = swap(shared, "expert")

    with jax.named_scope("backward"):
        (parcel,) = call(
            backward_kernel,
            [place],
            [shared, base_rows, facts, proj, slope, mod, head_all, rows]
            + weights,
            [((SHARDS, PACK, LANES), bf16)],
            fetch=(1, 2, 3, 4, 8, 9, 10, 11, 12, 5, 6, 7),
            flops=8 * D * HID * LANES,
        )
        parcel = swap(parcel, FSDP)
        (home,) = call(mid_kernel, [], [parcel], [((GROUPS, 16, LANES), bf16)])
        home = swap(home, "expert")

    with jax.named_scope("finish"):
        grad_tokens, loss = call(
            end_kernel,
            [place, levels],
            [home, pick],
            [((FEAT, TOK), bf16), ((1, 1), f32)],
        )
    return (grad_tokens.T, loss.reshape(()))


def solution(mesh):
    mesh = Mesh(mesh.devices.reshape(4, 2, 4, 16), FSDP + ("expert",))
    in_specs = (
        P("expert", FSDP),
        P(),
        P("expert", None),
        P("expert", None),
        P("expert", None, FSDP),
        P("expert", FSDP, None),
        P(None, FSDP),
        P("expert", None),
        P(),
        P(),
        P(),
    )
    out_specs = (P("expert", FSDP), P())
    return jax.shard_map(local, mesh=mesh, in_specs=in_specs, out_specs=out_specs, check_vma=False)
```

```python
import functools
import math

import jax
import jax.numpy as jnp
from jax import lax
from jax.experimental import pallas as pl
from jax.experimental.pallas import tpu as pltpu
from jax.sharding import Mesh, PartitionSpec as P

D = 1792
TOPK = 2
C_OUT = 16
SAMPLES = 4
LANES = 128
FEAT = 56
SHARDS = 32
GROUPS = 16
CAP = 32
TOK = 256
HID = 224
PACK = 64
FSDP = ("y", "zh", "zl")
RING = ("zh", "zl")
SHARERS = ("y", "zh")


norm_eps = 1e-06
dpo_beta = 2.0
bf16 = jnp.bfloat16
f32 = jnp.float32
i32 = jnp.int32
highest = lax.Precision.HIGHEST
contract_last = (((1,), (1,)), ((), ()))
contract_first = (((0,), (0,)), ((), ()))


def dot(a, b, **kw):
    return jnp.dot(a, b, preferred_element_type=f32, **kw)


def dot_nt(a, b, **kw):
    return lax.dot_general(a, b, contract_last, preferred_element_type=f32, **kw)


def iota(shape, axis):
    return lax.broadcasted_iota(i32, shape, axis)


def high_low(values):
    high = values.astype(bf16).astype(f32)
    return high, values - high


def whole(weight):
    if isinstance(weight, tuple):
        return jnp.concatenate([part[...] for part in weight], axis=0)
    return weight[...]


def lane_blocks(tiles):
    block = iota(tiles[0].shape, 1) // CAP
    out = []
    for b in range(4):
        total = None
        for j in range(4):
            moved = tiles[j] if j == b else pltpu.roll(tiles[j], (CAP * (j - b)) % LANES, axis=1)
            total = moved if total is None else jnp.where(block == j, moved, total)
        out.append(total)
    return out


def routing_kernel(place_ref, tokens_ref, routes_ref, weights_ref, targets_ref, sent_ref, pick_ref):
    shard = place_ref[0]
    expert = iota((GROUPS, TOK), 0)
    hits = [(routes_ref[k : k + 1, :] == expert).astype(f32) for k in range(TOPK)]
    below = (iota((TOK, TOK), 0) < iota((TOK, TOK), 1)).astype(bf16)
    named = hits[0] + hits[1]
    earlier = dot(named.astype(bf16), below)
    slots = [jnp.sum(earlier * hit, axis=0, keepdims=True) for hit in hits]
    kept = [(slot < CAP).astype(f32) for slot in slots]
    lost = (1.0 - kept[0]) * (1.0 - kept[1])
    rank = dot(jnp.broadcast_to(lost, (8, TOK)).astype(bf16), below)[0:1]
    full = jnp.minimum(jnp.sum(named, axis=1, keepdims=True), float(CAP))
    empty = jnp.broadcast_to(CAP - full, (GROUPS, LANES))
    order = (iota((GROUPS, GROUPS), 1) < iota((GROUPS, GROUPS), 0)).astype(bf16)
    start = dot(order, empty.astype(bf16))[:, 0:1]
    inside = (rank >= start) & (rank < start + CAP - full)
    spare = jnp.where(inside, expert.astype(f32) * CAP + full + rank - start, 0.0)
    spare = jnp.sum(spare, axis=0, keepdims=True)
    lane = iota((GROUPS * CAP, TOK), 0)
    places = []
    for k in range(TOPK):
        dest = routes_ref[k : k + 1, :].astype(f32) * CAP + slots[k]
        dest = jnp.where(kept[k] > 0.5, dest, -1.0)
        if k == 0:
            dest = jnp.where(lost > 0.5, spare, dest)
        places.append((lane == dest.astype(i32)).astype(f32))
    pick_ref[...] = (places[0] + places[1]).astype(bf16)
    pick_ref.start()

    row = iota((PACK, LANES), 0)
    pick_fact = ((row == FEAT) & (iota((PACK, LANES), 1) == shard)).astype(bf16)
    body = jnp.concatenate(
        [tokens_ref[...].astype(f32), jnp.zeros((PACK - FEAT, TOK), f32)], axis=0
    )
    line = iota((8, TOK), 0)
    packed = None
    for k in range(TOPK):
        other = 1 - k
        own = high_low(weights_ref[k : k + 1, :] * kept[k])
        partner = high_low(weights_ref[other : other + 1, :] * kept[other])
        first = jnp.ones((1, TOK), f32) if k == 0 else 1.0 - kept[0]
        facts = [
            own[0], own[1], partner[0], partner[1],
            routes_ref[other : other + 1, :].astype(f32) * kept[other],
            slots[other] * kept[other],
            first,
        ]
        table = jnp.zeros((8, TOK), f32)
        for place, fact in enumerate(facts):
            table = jnp.where(line == place, fact, table)
        table = jnp.concatenate(
            [targets_ref[...], table, jnp.zeros((LANES - C_OUT - 8, TOK), f32)], axis=0
        )
        features = body + dot(pick_fact, table.astype(bf16))
        part = dot_nt(features.astype(bf16), places[k].astype(bf16))
        packed = part if packed is None else packed + part
    for tile in range(4):
        pieces = [
            packed[16 * j : 16 * j + 16, tile * LANES : (tile + 1) * LANES] for j in range(4)
        ]
        for b, piece in enumerate(lane_blocks(pieces)):
            sent_ref[4 * tile + b] = piece.astype(bf16)


def parcel_kernel(arrived_ref, head_ref, parcel_ref):
    row = iota((8, LANES), 0)
    spread = jnp.concatenate([head_ref[...].astype(f32)] * 8, axis=0).T
    own = iota((FEAT, LANES), 1) // C_OUT == iota((FEAT, LANES), 0) % 8
    spread = jnp.where(own, spread, 0.0).astype(bf16)
    fold = iota((8, FEAT), 1) // 8 + 1 == iota((8, FEAT), 0)
    head = dot(fold.astype(bf16), spread)
    for q in range(4):
        tiles = lane_blocks([arrived_ref[4 * q + b].astype(f32) for b in range(4)])
        tail = jnp.where(row == 0, tiles[3][8:], head)
        body = jnp.concatenate([tiles[0], tiles[1], tiles[2], tiles[3][:8], tail], axis=0)
        body = body.astype(bf16)
        for high in range(8):
            parcel_ref[4 * high + q] = body


def head_kernel(gathered_ref, gate_ref, w_out_ref, proj_ref, head_ref):
    pieces = []
    for f in range(SHARDS):
        rows = gathered_ref[f, FEAT:PACK].astype(f32)
        for i in range(FEAT // 8):
            pieces.append(jnp.broadcast_to(rows[i + 1 : i + 2], (8, LANES)))
    spread = jnp.concatenate(pieces, axis=0)
    lane = iota((D, LANES), 1)
    spread = jnp.where(lane // C_OUT == iota((D, LANES), 0) % 8, spread, 0.0).astype(bf16)
    fold = iota((LANES, LANES), 0) % C_OUT == iota((LANES, LANES), 1) % C_OUT
    head = dot(spread, fold.astype(bf16))
    head_ref[...] = head.astype(bf16)
    head_ref.start()
    high, low = high_low(head * gate_ref[...])
    pair = jnp.where(lane < PACK, high, low).astype(bf16)
    proj = dot(w_out_ref[...], pair)
    proj = proj + pltpu.roll(proj, PACK, axis=1)
    proj = proj.T
    for z in range(8):
        q = z % SAMPLES
        proj_ref[z] = proj[C_OUT * q : C_OUT * (q + 1)].astype(bf16)


def first_kernel(
    place_ref, gathered_ref, mod_ref, w0_ref, w1_ref, w2_ref, w3_ref, w4_ref, head_ref,
    act_ref, slope_ref, rows_ref, base_ref, facts_ref,
):
    rows = jnp.concatenate([gathered_ref[f, :FEAT].astype(f32) for f in range(SHARDS)], axis=0).T
    rows_ref[...] = rows.astype(bf16)
    rows_ref.start()
    rms = lax.rsqrt(jnp.sum(rows * rows, axis=1, keepdims=True) / D + norm_eps)
    mine = pl.ds(place_ref[1], 1)
    normed = (rows * rms) * (1.0 + mod_ref[1, mine, :]) + mod_ref[0, mine, :]
    normed = normed.astype(bf16)
    weights = [w0_ref, w1_ref, w2_ref, (w3_ref, w4_ref)]
    for b, weight in enumerate(weights):
        pre = dot_nt(normed, whole(weight))
        cubic = math.sqrt(2.0 / math.pi)
        square = pre * pre
        tanh = jnp.tanh(cubic * (pre + 0.044715 * square * pre))
        half = 0.5 * (1.0 + tanh)
        act_ref[b] = (pre * half).astype(bf16)
        slope_ref[b] = half + 0.5 * pre * (1.0 - tanh * tanh) * (
            cubic * (1.0 + 3.0 * 0.044715 * square)
        )
        slope_ref.start(b)
    base_ref[...] = dot(rows.astype(bf16), head_ref[...]).T[:C_OUT]
    tails = [gathered_ref[f, FEAT:PACK].astype(f32)[:1] for f in range(SHARDS)]
    facts_ref[...] = jnp.concatenate(tails, axis=0)


def held_projections(proj_ref, z):
    lane = iota((C_OUT, HID), 1)
    after, before = proj_ref[(z + 2) % 8].astype(f32), proj_ref[(z + 6) % 8].astype(f32)
    ends = jnp.where(lane < HID // 2, after, before).astype(bf16)
    return [proj_ref[z], proj_ref[(z + 7) % 8], proj_ref[(z + 1) % 8], ends]


def predict_kernel(place_ref, act_ref, proj_ref, part_ref):
    total = None
    for b, proj in enumerate(held_projections(proj_ref, place_ref[4])):
        part = dot_nt(proj, act_ref[b])
        total = part if total is None else total + part
    for other in range(8):
        part_ref[other] = total


def own_kernel(parts_ref, shared_ref):
    own = jnp.sum(parts_ref[...], axis=0).astype(bf16)
    for e in range(GROUPS):
        shared_ref[e] = own


def backward_kernel(
    place_ref, shared_ref, base_ref, facts_ref, proj_ref, slope_ref,
    mod_ref, head_ref, rows_ref, w0_ref, w1_ref, w2_ref, w3_ref, w4_ref, parcel_ref,
):
    quarter, leader = place_ref[1], place_ref[2]
    facts = facts_ref[...]
    target = facts[:C_OUT]
    own_w = facts[16:17] + facts[17:18]
    other_w = facts[18:19] + facts[19:20]
    first = facts[22:23]
    lane = iota((1, LANES), 1)
    source = facts[20:21].astype(i32) * LANES + facts[21:22].astype(i32) + lane // CAP * CAP
    chosen = (iota((GROUPS * LANES, LANES), 0) == source).astype(f32).astype(bf16)
    everyone = jnp.concatenate([shared_ref[e] for e in range(GROUPS)], axis=1)
    partner = dot(everyone, chosen)
    residue = base_ref[...] + own_w * shared_ref[place_ref[5]].astype(f32) + other_w * partner - target
    kept_err = jnp.sum(first * residue * residue, keepdims=True)

    err = jnp.where((lane == quarter) & (leader == 1), kept_err, 0.0)
    row = iota((8, LANES), 0)
    tail = jnp.zeros((8, LANES), f32)
    for place, values in enumerate(high_low(err)):
        tail = jnp.where(row == place, values, tail)

    upstream = jnp.concatenate(high_low((own_w * residue).T), axis=1).astype(bf16)
    weights = [w0_ref, w1_ref, w2_ref, (w3_ref, w4_ref)]
    total = None
    for b, proj in enumerate(held_projections(proj_ref, place_ref[4])):
        grad = slope_ref[b] * dot(upstream, jnp.concatenate([proj, proj], axis=0))
        part = dot(grad.astype(bf16), whole(weights[b]))
        total = part if total is None else total + part
    rows = rows_ref[...].astype(f32)
    rms = lax.rsqrt(jnp.sum(rows * rows, axis=1, keepdims=True) / D + norm_eps)
    total = total * (rms * (1.0 + mod_ref[1, pl.ds(quarter, 1), :]))
    inner = jnp.sum(total * rows, axis=1, keepdims=True) * (rms * rms / D)
    high, low = high_low(first * residue * 0.125)
    direct = jnp.concatenate([high, low, jnp.zeros((LANES - 2 * C_OUT, LANES), f32)], axis=0)
    total = total - rows * inner + dot_nt(direct.T.astype(bf16), head_ref[...])
    total = total.T
    for f in range(SHARDS):
        parcel_ref[f] = jnp.concatenate(
            [total[FEAT * f : FEAT * (f + 1)], tail], axis=0
        ).astype(bf16)


def mid_kernel(parcel_ref, home_ref):
    lane = iota((1, LANES), 1)
    row = iota((8, LANES), 0)
    sums, tails = [], []
    for q in range(4):
        total = None
        for high in range(8):
            f = 4 * high + q
            part = parcel_ref[f].astype(f32)
            total = part if total is None else total + part
        sums.append(total[:FEAT])
        tails.append(total[FEAT:])
    tail = tails[0] + tails[1] + tails[2] + tails[3]
    err = jnp.where(lane < SAMPLES, tail[0:1] + tail[1:2], 0.0)
    err = err + pltpu.roll(err, CAP, axis=1)
    err = err + pltpu.roll(err, 2 * CAP, axis=1)
    high, low = high_low(err)
    tail = jnp.where(row == 0, high, 0.0) + jnp.where(row == 1, low, 0.0)
    for q in range(4):
        full = jnp.concatenate([sums[q], tail], axis=0)
        tiles = lane_blocks([full[16 * j : 16 * j + 16] for j in range(4)])
        for b in range(4):
            home_ref[4 * q + b] = tiles[b].astype(bf16)


def end_kernel(
    place_ref, levels_ref, home_ref, pick_ref,
    grad_ref, loss_ref,
):
    sample = place_ref[3].astype(f32)
    pairs = [levels_ref[SAMPLES + 2 + i] for i in range(SAMPLES)]
    columns = []
    for tile in range(4):
        tiles = lane_blocks([home_ref[4 * tile + b].astype(f32) for b in range(4)])
        columns.append(jnp.concatenate(tiles, axis=0))
    home = jnp.concatenate(columns, axis=1)
    back = dot(home.astype(bf16), pick_ref[...])
    err = functools.reduce(jnp.add, [column[FEAT : FEAT + 1] for column in columns])
    err = err + functools.reduce(jnp.add, [column[FEAT + 1 : FEAT + 2] for column in columns])
    err = jnp.broadcast_to(err, (8, LANES)) / (TOK * GROUPS // SAMPLES * C_OUT)
    lane = iota((8, LANES), 1) % CAP
    excess = []
    for s in range(SAMPLES):
        total = jnp.sum(jnp.where(lane == s, err, 0.0), axis=1, keepdims=True)
        excess.append(jnp.broadcast_to(total, (8, LANES)) - levels_ref[s])
    loss, coef = 0.0, 0.0
    for k in range(2):
        winner, loser = pairs[2 * k], pairs[2 * k + 1]
        margin = 0.0
        for s in range(SAMPLES):
            margin = margin + jnp.where(winner == s, excess[s], 0.0)
        for s in range(SAMPLES):
            margin = margin - jnp.where(loser == s, excess[s], 0.0)
        down = levels_ref[SAMPLES + k] * margin
        loss = loss + jnp.maximum(down, 0.0) + jnp.log1p(jnp.exp(-jnp.abs(down)))
        rate = levels_ref[SAMPLES + k] / (1.0 + jnp.exp(-down)) * 0.5
        coef = coef + jnp.where(winner == sample, rate, 0.0)
        coef = coef - jnp.where(loser == sample, rate, 0.0)
    loss_ref[...] = loss[0:1, 0:1] * 0.5
    coef = coef[0:1, 0:1] * (TOK * GROUPS * C_OUT * 2.0 / (TOK * GROUPS // SAMPLES * C_OUT))
    grad_ref[...] = (coef * back[:FEAT]).astype(bf16)


class Fetched:
    def __init__(self, source, held, semaphore):
        self.held = held
        self.copy = pltpu.make_async_copy(source, held, semaphore)
        self.copy.start()

    def wait(self):
        if self.copy is not None:
            self.copy.wait()
            self.copy = None

    def __getitem__(self, index):
        self.wait()
        return self.held[index]


class Stored:
    def __init__(self, target, held, semaphore, parts):
        self.held = held
        if parts == 1:
            self.copies = [pltpu.make_async_copy(held, target, semaphore.at[0])]
        else:
            self.copies = [
                pltpu.make_async_copy(held.at[i], target.at[i], semaphore.at[i])
                for i in range(parts)
            ]
        self.started = [False] * parts

    def __setitem__(self, index, values):
        self.held[index] = values

    def start(self, part=0):
        if not self.started[part]:
            self.copies[part].start()
            self.started[part] = True

    def finish(self):
        for part in range(len(self.copies)):
            self.start(part)

    def wait(self):
        for copy in self.copies:
            copy.wait()


def call(kernel, scalars, arrays, outs, fetch=(), store=(), parts={}, flops=0):
    vmem = pl.BlockSpec(memory_space=pltpu.VMEM)
    smem = pl.BlockSpec(memory_space=pltpu.SMEM)
    hbm = pl.BlockSpec(memory_space=pltpu.HBM)
    size = sum(a.size * a.dtype.itemsize for a in arrays)
    out_shape = [
        pltpu.HBM(shape, dtype) if i in store else jax.ShapeDtypeStruct(shape, dtype)
        for i, (shape, dtype) in enumerate(outs)
    ]
    arrays = [
        pltpu.with_memory_space_constraint(a, pltpu.HBM) if i in fetch else a
        for i, a in enumerate(arrays)
    ]
    moved = [arrays[i] for i in fetch] + [out_shape[i] for i in store]
    scratch = [pltpu.VMEM(a.shape, a.dtype) for a in moved]
    counts = [1] * len(fetch) + [parts.get(i, 1) for i in store]
    starts = [sum(counts[:n]) for n in range(len(counts))]
    if moved:
        scratch.append(pltpu.SemaphoreType.DMA((sum(counts),)))

    def body(*refs):
        refs = list(refs)
        at_in = len(scalars)
        at_out = at_in + len(arrays)
        at_held = at_out + len(outs)
        fetched, stored = [], []
        for n, i in enumerate(fetch):
            fetched.append(Fetched(refs[at_in + i], refs[at_held + n], refs[-1].at[n]))
            refs[at_in + i] = fetched[-1]
        for n, i in enumerate(store, len(fetch)):
            semaphores = refs[-1].at[pl.ds(starts[n], counts[n])]
            stored.append(Stored(refs[at_out + i], refs[at_held + n], semaphores, counts[n]))
            refs[at_out + i] = stored[-1]
        kernel(*refs[:at_held])
        for item in stored:
            item.finish()
        for item in fetched + stored:
            item.wait()

    return pl.pallas_call(
        body,
        out_shape=out_shape,
        in_specs=[smem] * len(scalars)
        + [hbm if i in fetch else vmem for i in range(len(arrays))],
        out_specs=[hbm if i in store else vmem for i in range(len(outs))],
        scratch_shapes=scratch,
        compiler_params=pltpu.CompilerParams(vmem_limit_bytes=24 * 1024 * 1024),
        cost_estimate=pl.CostEstimate(flops=flops, bytes_accessed=size, transcendentals=0),
    )(*scalars, *arrays)


def swap(chunks, axis):
    return lax.all_to_all(chunks, axis, split_axis=0, concat_axis=0, tiled=True)


def local(
    tokens,
    modulation,
    routes,
    route_weights,
    w_first,
    w_second,
    head,
    targets,
    ref_err,
    pair_ids,
    timesteps,
):
    shard = lax.axis_index(FSDP)
    ring = lax.axis_index(RING)
    quarter = lax.axis_index("zl")
    leader = (lax.axis_index(SHARERS) == 0).astype(i32)
    my_sample = lax.axis_index("expert") * SAMPLES // GROUPS
    place = jnp.stack([shard, quarter, leader, my_sample, ring, lax.axis_index("expert")]).astype(i32)
    fraction = timesteps.astype(f32) / 1000.0
    keep_level = jnp.cos((fraction + 0.008) / 1.008 * (math.pi / 2.0)) ** 2
    levels = jnp.concatenate([ref_err, dpo_beta * keep_level, pair_ids.astype(f32)])
    w_in = w_first[0].T
    mod = modulation.transpose(1, 0, 2)

    with jax.named_scope("weights"):
        up = [(z, (z + 1) % 8) for z in range(8)]
        down = [(z, (z + 7) % 8) for z in range(8)]
        w_before = lax.ppermute(w_in, RING, up)
        w_after = lax.ppermute(w_in, RING, down)

    with jax.named_scope("routing"):
        sent, pick = call(
            routing_kernel,
            [place],
            [tokens.T, routes.T, route_weights.T, targets.T],
            [((GROUPS, 16, LANES), bf16), ((GROUPS * CAP, TOK), bf16)],
            store=(1,),
        )
    with jax.named_scope("dispatch"):
        arrived = swap(sent, "expert")
        (parcel,) = call(parcel_kernel, [], [arrived, head], [((SHARDS, PACK, LANES), bf16)])
        parcel, w_before, w_after = lax.optimization_barrier((parcel, w_before, w_after))
        half = HID // 2
        weights = [
            w_in,
            w_before,
            w_after,
            lax.ppermute(w_after[:half], RING, down),
            lax.ppermute(w_before[half:], RING, up),
        ]
        gathered, levels = lax.optimization_barrier((swap(parcel, FSDP), levels))

    with jax.named_scope("projection"):
        gate = jnp.tile(jnp.repeat(mod[2].T, C_OUT, axis=1), (1, 2))
        proj, head_all = call(
            head_kernel,
            [],
            [gathered, gate, w_second[0]],
            [((8, C_OUT, HID), bf16), ((D, LANES), bf16)],
            store=(0, 1),
        )
        proj = swap(proj, RING)

    with jax.named_scope("first_layer"):
        act, slope, rows, base_rows, facts = call(
            first_kernel,
            [place],
            [gathered, mod] + weights + [head_all],
            [((4, LANES, HID), bf16), ((4, LANES, HID), f32), ((LANES, D), bf16), ((C_OUT, LANES), f32), ((SHARDS, LANES), f32)],
            fetch=(1, 2, 3, 4, 7),
            store=(1, 2, 3, 4),
            parts={1: 4},
            flops=8 * D * HID * LANES,
        )

    with jax.named_scope("predict"):
        (part,) = call(
            predict_kernel, [place], [act, proj], [((8, C_OUT, LANES), f32)]
        )
        parts = swap(part, SHARERS)
        (shared,) = call(own_kernel, [], [parts], [((GROUPS, C_OUT, LANES), bf16)])
        shared = swap(shared, "expert")

    with jax.named_scope("backward"):
        (parcel,) = call(
            backward_kernel,
            [place],
            [shared, base_rows, facts, proj, slope, mod, head_all, rows]
            + weights,
            [((SHARDS, PACK, LANES), bf16)],
            fetch=(1, 2, 3, 4, 8, 9, 10, 11, 12, 5, 6, 7),
            flops=8 * D * HID * LANES,
        )
        parcel = swap(parcel, FSDP)
        (home,) = call(mid_kernel, [], [parcel], [((GROUPS, 16, LANES), bf16)])
        home = swap(home, "expert")

    with jax.named_scope("finish"):
        grad_tokens, loss = call(
            end_kernel,
            [place, levels],
            [home, pick],
            [((FEAT, TOK), bf16), ((1, 1), f32)],
        )
    return (grad_tokens.T, loss.reshape(()))


def solution(mesh):
    mesh = Mesh(mesh.devices.reshape(4, 2, 4, 16), FSDP + ("expert",))
    in_specs = (
        P("expert", FSDP),
        P(),
        P("expert", None),
        P("expert", None),
        P("expert", None, FSDP),
        P("expert", FSDP, None),
        P(None, FSDP),
        P("expert", None),
        P(),
        P(),
        P(),
    )
    out_specs = (P("expert", FSDP), P())
    return jax.shard_map(local, mesh=mesh, in_specs=in_specs, out_specs=out_specs, check_vma=False)
```
